128 devices in a mesh: pair: 8 (over y, core), virt: 16 (over x, z).
Axes of the slice: x: 4, y: 4, z: 4, core: 2. Of those that a mesh axis runs over, the one named last changes fastest.
Arguments:
- amplitudes: bfloat16 [2048, 16384], P(('pair', 'virt')), may hold values from -6 to 6
- tile_irreps: int32 [128], replicated, may hold values from 0 to 3, as said below
- ladder_blocks: bfloat16 [16384, 6144], P('virt'), as said below
Outputs:
- ladder_residual: bfloat16 [2048, 16384], P(('pair', 'virt'))
The draws below stay inside these ranges and needn't reach their ends.
Inputs may be any that keep to these rules, and one draw needn't show every extreme that they name: `tile_irreps`: Non-decreasing along the tiles; each irrep holds at most 48 tiles and one holds exactly 48. Symmetric within an irrep: for pairs u and v of the same irrep g with u - first_g * 128 = j and v - first_g * 128 = k, ladder_blocks[u, k] == ladder_blocks[v, j]. Columns at or beyond count_g * 128 for rows of irrep g are not part of the operator.
All inputs are finite; a program needn't handle non-finite values.
Results may differ from the reference program's by a relative error of at most 0.0051.
Values may be sent and summed in bfloat16 or wider, within the bound.
No kernel may reach another device: no remote copies, remote signals or barrier semaphores. Data moves between devices by JAX's collectives and lax.ppermute only.
A program may use at most 192 MiB of HBM per device.

```python
import jax
import jax.numpy as jnp
from jax import lax

TILE = 128
NT_TILES = 128
SECT = 48
ROWS = 2048


def sector_labels(key):
    key = jax.random.fold_in(key, 101)
    first_key, second_key, third_key = jax.random.split(key, 3)
    rest = NT_TILES - SECT
    lowest = rest // 6
    first_lo = max(lowest, rest - 2 * SECT)
    first_len = jax.random.randint(first_key, (), first_lo, min(SECT, rest - 2 * lowest) + 1)
    second_lo = jnp.maximum(lowest, rest - first_len - SECT)
    second_hi = jnp.minimum(SECT, rest - first_len - lowest)
    second_len = jax.random.randint(second_key, (), second_lo, second_hi + 1)
    third_len = rest - first_len - second_len
    biggest = jax.random.randint(third_key, (), 0, 4)
    others = jnp.stack([first_len, second_len, third_len]).astype(jnp.int32)
    irreps = jnp.arange(4, dtype=jnp.int32)
    picked = jnp.clip(irreps - (irreps > biggest).astype(jnp.int32), 0, 2)
    lengths = jnp.where(irreps == biggest, SECT, others[picked]).astype(jnp.int32)
    ends = jnp.cumsum(lengths)
    tiles = jnp.arange(NT_TILES, dtype=jnp.int32)
    return jnp.sum((tiles[:, None] >= ends[None, :]).astype(jnp.int32), axis=1).astype(jnp.int32)


def draw_tile_irreps(key, part):
    return sector_labels(key)


def draw_ladder_blocks(key, part):
    labels = sector_labels(key)
    key = jax.random.fold_in(key, 7)
    window = SECT * TILE
    total_rows = NT_TILES * TILE
    base = jax.random.normal(key, (total_rows, window), jnp.float32)
    irreps = jnp.arange(4, dtype=jnp.int32)
    lengths = jnp.sum((labels[None, :] == irreps[:, None]).astype(jnp.int32), axis=1)
    starts = jnp.cumsum(lengths) - lengths
    row_ids = jnp.arange(total_rows, dtype=jnp.int32)
    row_start = (starts[labels[row_ids // TILE]] * TILE).astype(jnp.int32)
    offsets = jnp.arange(window, dtype=jnp.int32)
    mirror_row = jnp.clip(row_start[:, None] + offsets[None, :], 0, total_rows - 1)
    mirror_col = jnp.clip((row_ids - row_start)[:, None], 0, window - 1)
    flat_index = mirror_row * window + mirror_col
    mirrored = jnp.take(base.reshape(-1), flat_index.reshape(-1)).reshape(total_rows, window)
    scale = 0.5 ** 0.5 / window ** 0.5
    return ((base + mirrored) * scale).astype(jnp.bfloat16)


def steps_of(stream_key, dims, shards, smallest, high):
    factor_of, own = 1.0, jax.random.fold_in(stream_key, 6)
    for axis_at, shards_of in shards:
        steps = jnp.exp(jax.random.uniform(jax.random.fold_in(own, axis_at), (shards_of,), jnp.float32, smallest / len(shards), high / len(shards)))
        factor_of = factor_of * jnp.repeat(steps, dims[axis_at] // shards_of).reshape([-1 if axis == axis_at else 1 for axis in range(len(dims))])
    return factor_of


def centred(own_key, shape, scale, most, shards=(), kind=jnp.bfloat16):
    array = jax.random.normal(own_key, shape, jnp.float32) * scale
    if len(shards) > 0:
        array = steps_of(own_key, shape, shards, -0.22, 0.18) * array
    return jnp.clip(array, min=-most, max=most).astype(kind)


def setup_inputs(seed: int = 0) -> dict:
    keys = jax.random.split(jax.random.key(seed), 4)
    return {
        "amplitudes": centred(keys[0], (ROWS, NT_TILES * TILE), 1.0, 6.0, ((0, 128),)),
        "tile_irreps": draw_tile_irreps(jax.random.fold_in(keys[3], 71), 0),
        "ladder_blocks": draw_ladder_blocks(jax.random.fold_in(keys[3], 71), 0),
    }


def sector_table(tile_irreps):
    irreps = jnp.arange(4, dtype=jnp.int32)
    lengths = jnp.sum((tile_irreps[None, :] == irreps[:, None]).astype(jnp.int32), axis=1).astype(jnp.int32)
    starts = (jnp.cumsum(lengths) - lengths).astype(jnp.int32)
    return starts, lengths


def reference(amplitudes, tile_irreps, ladder_blocks):
    rows, width = amplitudes.shape
    half = rows // 2
    window = ladder_blocks.shape[1]
    upper_rows = amplitudes[:half].astype(jnp.float32)
    lower_rows = amplitudes[half:].astype(jnp.float32)
    tau = (0.5 * (upper_rows - lower_rows)).astype(jnp.bfloat16)
    starts, lengths = sector_table(tile_irreps)
    offsets = jnp.arange(window, dtype=jnp.int32)

    def step(total, tile_id):
        irrep = tile_irreps[tile_id]
        columns = lax.dynamic_slice_in_dim(tau, tile_id * TILE, TILE, 1)
        block = lax.dynamic_slice_in_dim(ladder_blocks, tile_id * TILE, TILE, 0)
        contrib = jnp.dot(columns, block, preferred_element_type=jnp.float32)
        contrib = jnp.where(offsets[None, :] < lengths[irrep] * TILE, contrib, jnp.zeros_like(contrib))
        place = starts[irrep] * TILE
        current = lax.dynamic_slice_in_dim(total, place, window, 1)
        return lax.dynamic_update_slice_in_dim(total, current + contrib, place, 1), None

    total, unused = lax.scan(step, jnp.zeros((half, width + window), jnp.float32), jnp.arange(width // TILE, dtype=jnp.int32))
    upper_out = total[:, :width].astype(jnp.bfloat16)
    return jnp.concatenate([upper_out, -upper_out], axis=0)
```

```python
import functools

import jax
import jax.numpy as jnp
from jax import lax
from jax.experimental import pallas as pl
from jax.experimental.pallas import tpu as pltpu
from jax.sharding import Mesh, PartitionSpec as P

TILE = 128
IRREPS = 4
TILES = 128
SECT = 48
OWNED = 8
VIRT = 16
ROWS = 8
EXTRA = 5
SLOTS = SECT + EXTRA
SIDE = 4
OUT_SLOTS = OWNED + 2 * SIDE
MAIN = 8


def clip_count(first, count, w):
    low, high = jnp.maximum(first, w * OWNED), jnp.minimum(first + count, w * OWNED + OWNED)
    return jnp.maximum(high - low, 0)


def plan_kernel(irreps_ref, table_ref):
    def count(at, counts):
        irrep = irreps_ref[at]
        return tuple(counts[g] + (irrep == g).astype(jnp.int32) for g in range(IRREPS))

    counts = lax.fori_loop(0, TILES, count, (jnp.int32(0),) * IRREPS)
    first = jnp.int32(0)
    firsts = []
    for g in range(IRREPS):
        firsts.append(first)
        table_ref[g] = first
        table_ref[IRREPS + g] = counts[g]
        first = first + counts[g]
    for w in range(VIRT):
        best, main = clip_count(firsts[0], counts[0], w), jnp.int32(0)
        for g in range(1, IRREPS):
            held = clip_count(firsts[g], counts[g], w)
            main = jnp.where(held > best, g, main)
            best = jnp.maximum(held, best)
        table_ref[MAIN + w] = main


def plan(tile_irreps):
    return pl.pallas_call(
        plan_kernel,
        out_shape=jax.ShapeDtypeStruct((32,), jnp.int32),
        in_specs=[pl.BlockSpec(memory_space=pltpu.SMEM)],
        out_specs=pl.BlockSpec(memory_space=pltpu.SMEM),
        name="plan",
    )(tile_irreps)


def position(table_ref, w):
    main = table_ref[MAIN + w]
    first, count = table_ref[main], table_ref[IRREPS + main]
    before = jnp.maximum(first - w * OWNED, 0)
    return main, first, count, before, clip_count(first, count, w)


def pack_kernel(table_ref, place_ref, own_ref, partner_ref, out_ref, tau_ref):
    lower = place_ref[0] == 1
    for tile in range(TILES):
        columns = pl.ds(tile * TILE, TILE)
        own = own_ref[:, columns].astype(jnp.float32)
        mine = jnp.where(lower, own[ROWS:], own[:ROWS])
        other = partner_ref[:, columns].astype(jnp.float32)
        tau_ref[tile] = (0.5 * (mine - other)).astype(jnp.bfloat16)
    tau_ref[TILES] = jnp.zeros((ROWS, TILE), jnp.bfloat16)

    @pl.loop(0, VIRT)
    def _(w):
        _, first, count, before, held = position(table_ref, w)
        for slot in range(SECT):
            out_ref[w, slot] = tau_ref[jnp.where(slot < count, first + slot, TILES)]
        for extra in range(EXTRA):
            at = jnp.where(extra < before, extra, extra + held)
            at = jnp.where(at < OWNED, w * OWNED + at, TILES)
            out_ref[w, SECT + extra] = tau_ref[at]


def pack(table, place, own, partner):
    return pl.pallas_call(
        pack_kernel,
        out_shape=jax.ShapeDtypeStruct((VIRT, SLOTS, ROWS, TILE), jnp.bfloat16),
        in_specs=[pl.BlockSpec(memory_space=pltpu.SMEM)] * 2 + [pl.BlockSpec(memory_space=pltpu.VMEM)] * 2,
        out_specs=pl.BlockSpec(memory_space=pltpu.VMEM),
        scratch_shapes=[pltpu.VMEM((TILES + 1, ROWS, TILE), jnp.bfloat16)],
        compiler_params=pltpu.CompilerParams(vmem_limit_bytes=40 << 20),
        name="pack",
    )(table, place, own, partner)


GROUP = 2
NT = (((1,), (1,)), ((), ()))
NN = (((1,), (0,)), ((), ()))


def right_start(first, last_block):
    return jnp.minimum(last_block * OWNED - first, SECT - SIDE)


def ladder_kernel(
    table_ref, place_ref, irreps_ref, tau_ref, block_ref, out_ref, held_ref, left_ref, right_ref, own_ref, total_ref
):
    step = pl.program_id(0)
    w = place_ref[1]
    main, first, _, before, held = position(table_ref, w)

    @pl.when(step == 0)
    def _():
        for slot in range(SLOTS):
            for src in range(0, VIRT, 2):
                rows = jnp.concatenate([tau_ref[src, slot], tau_ref[src + 1, slot]], axis=0)
                held_ref[pl.ds(src * ROWS, 2 * ROWS), pl.ds(slot * TILE, TILE)] = rows
        left_ref[...] = jnp.zeros_like(left_ref)
        right_ref[...] = jnp.zeros_like(right_ref)

    def tau_of(tile):
        inside = w * OWNED + tile - first
        outside = SECT + jnp.where(tile < before, tile, tile - held)
        slot = jnp.where(irreps_ref[w * OWNED + tile] == main, inside, outside)
        return held_ref[:, pl.ds(pl.multiple_of(slot * TILE, TILE), TILE)]

    def send(slot, values):
        values = values.astype(jnp.bfloat16)
        for dest in range(VIRT):
            rows = values[dest * ROWS : (dest + 1) * ROWS]
            out_ref[dest, slot] = rows
            out_ref[VIRT + dest, slot] = rows

    total_ref[...] = lax.dot_general(
        held_ref[:, : SECT * TILE], block_ref[...], NT, preferred_element_type=jnp.float32
    )
    left_irrep = irreps_ref[w * OWNED]
    left_first = table_ref[left_irrep]
    left_block = left_first // OWNED
    left_on = (left_block != w) & (table_ref[MAIN + left_block] != left_irrep)
    right_irrep = irreps_ref[w * OWNED + OWNED - 1]
    right_first = table_ref[right_irrep]
    right_block = (right_first + table_ref[IRREPS + right_irrep] - 1) // OWNED
    right_on = (right_block != w) & (table_ref[MAIN + right_block] != right_irrep)
    for part in range(GROUP):
        tile = step * GROUP + part
        rows = pl.ds(part * TILE, TILE)
        irrep = irreps_ref[w * OWNED + tile]
        own_ref[...] = total_ref[:, part * TILE : (part + 1) * TILE]

        @pl.when(irrep != main)
        def _():
            own_ref[...] = jnp.zeros_like(own_ref)

            @pl.loop(0, OWNED)
            def _(other):
                @pl.when(irreps_ref[w * OWNED + other] == irrep)
                def _():
                    at = (w * OWNED + other - table_ref[irrep]) * TILE
                    own_ref[...] += lax.dot_general(
                        tau_of(other),
                        block_ref[rows, pl.ds(pl.multiple_of(at, TILE), TILE)],
                        NT,
                        preferred_element_type=jnp.float32,
                    )

        send(tile, own_ref[...])

        @pl.when(left_on & (irrep == left_irrep))
        def _():
            left_ref[...] += lax.dot_general(
                tau_of(tile), block_ref[rows, : SIDE * TILE], NN, preferred_element_type=jnp.float32
            )

        @pl.when(right_on & (irrep == right_irrep))
        def _():
            at = pl.multiple_of(right_start(right_first, right_block) * TILE, TILE)
            right_ref[...] += lax.dot_general(
                tau_of(tile), block_ref[rows, pl.ds(at, SIDE * TILE)], NN, preferred_element_type=jnp.float32
            )

    @pl.when(step == OWNED // GROUP - 1)
    def _():
        for side in range(SIDE):
            send(OWNED + side, left_ref[:, side * TILE : (side + 1) * TILE])
            send(OWNED + SIDE + side, right_ref[:, side * TILE : (side + 1) * TILE])


def ladder(table, place, tile_irreps, taken, blocks):
    rows = VIRT * ROWS
    window = SECT * TILE
    return pl.pallas_call(
        ladder_kernel,
        out_shape=jax.ShapeDtypeStruct((2 * VIRT, OUT_SLOTS, ROWS, TILE), jnp.bfloat16),
        grid_spec=pltpu.PrefetchScalarGridSpec(
            num_scalar_prefetch=3,
            grid=(OWNED // GROUP,),
            in_specs=[
                pl.BlockSpec((VIRT, SLOTS, ROWS, TILE), lambda i, *_: (0, 0, 0, 0)),
                pl.BlockSpec((GROUP * TILE, window), lambda i, *_: (i, 0)),
            ],
            out_specs=pl.BlockSpec((2 * VIRT, OUT_SLOTS, ROWS, TILE), lambda i, *_: (0, 0, 0, 0)),
            scratch_shapes=[
                pltpu.VMEM((rows, SLOTS * TILE), jnp.bfloat16),
                pltpu.VMEM((rows, SIDE * TILE), jnp.float32),
                pltpu.VMEM((rows, SIDE * TILE), jnp.float32),
                pltpu.VMEM((rows, TILE), jnp.float32),
                pltpu.VMEM((rows, GROUP * TILE), jnp.float32),
            ],
        ),
        compiler_params=pltpu.CompilerParams(vmem_limit_bytes=48 << 20),
        cost_estimate=pl.CostEstimate(
            flops=2 * rows * window * OWNED * TILE, bytes_accessed=16 << 20, transcendentals=0
        ),
        name="ladder",
    )(table, place, tile_irreps, taken, blocks)


def collect_kernel(table_ref, place_ref, irreps_ref, taken_ref, out_ref):
    lower = place_ref[0] == 1
    signs = (jnp.where(lower, -1.0, 1.0), jnp.where(lower, 1.0, -1.0))

    @pl.loop(0, VIRT)
    def _(w):
        for tile in range(OWNED):
            both = [taken_ref[half * VIRT + w, tile].astype(jnp.float32) * signs[half] for half in range(2)]
            columns = pl.ds(pl.multiple_of((w * OWNED + tile) * TILE, TILE), TILE)
            out_ref[:, columns] = jnp.concatenate(both, axis=0).astype(jnp.bfloat16)
        main, _, _, _, held = position(table_ref, w)

        @pl.when(held < OWNED)
        def _():
            @pl.loop(0, OWNED)
            def _(tile):
                at = w * OWNED + tile
                irrep = irreps_ref[at]

                @pl.when(irrep != main)
                def _():
                    first = table_ref[irrep]
                    left_block = first // OWNED
                    right_block = (first + table_ref[IRREPS + irrep] - 1) // OWNED
                    on_left = w == left_block
                    low = jnp.where(on_left, left_block + 1, left_block)
                    high = jnp.where(on_left, right_block + 1, right_block)
                    slot = jnp.where(
                        on_left,
                        OWNED + at - first,
                        OWNED + SIDE + at - first - right_start(first, right_block),
                    )
                    both = []
                    for half in range(2):
                        total = lax.fori_loop(
                            low,
                            high,
                            lambda v, total: total + taken_ref[half * VIRT + v, slot].astype(jnp.float32),
                            taken_ref[half * VIRT + w, tile].astype(jnp.float32),
                        )
                        both.append(total * signs[half])
                    columns = pl.ds(pl.multiple_of(at * TILE, TILE), TILE)
                    out_ref[:, columns] = jnp.concatenate(both, axis=0).astype(jnp.bfloat16)


def collect(table, place, tile_irreps, taken):
    return pl.pallas_call(
        collect_kernel,
        out_shape=jax.ShapeDtypeStruct((2 * ROWS, TILES * TILE), jnp.bfloat16),
        in_specs=[pl.BlockSpec(memory_space=pltpu.SMEM)] * 3 + [pl.BlockSpec(memory_space=pltpu.VMEM)],
        out_specs=pl.BlockSpec(memory_space=pltpu.VMEM),
        compiler_params=pltpu.CompilerParams(vmem_limit_bytes=40 << 20),
        name="collect",
    )(table, place, tile_irreps, taken)


def on_device(amplitudes, tile_irreps, ladder_blocks):
    half = lax.axis_index("half")
    place = jnp.stack([half, lax.axis_index("virt")]).astype(jnp.int32)
    sent = lax.dynamic_slice_in_dim(amplitudes, (1 - half) * ROWS, ROWS, 0)
    partner = lax.ppermute(sent, "half", [(0, 1), (1, 0)])
    table = plan(tile_irreps)
    packed = pack(table, place, amplitudes, partner)
    taken = lax.all_to_all(packed, "virt", split_axis=0, concat_axis=0, tiled=True)
    sums = ladder(table, place, tile_irreps, taken, ladder_blocks)
    taken = lax.all_to_all(sums, ("half", "virt"), split_axis=0, concat_axis=0, tiled=True)
    return collect(table, place, tile_irreps, taken)


def solution(mesh):
    pairs, virt = mesh.devices.shape
    split = Mesh(mesh.devices.reshape(2, pairs // 2, virt), ("half", "quarter", "virt"))
    rows = P(("half", "quarter", "virt"), None)
    return jax.shard_map(
        on_device, mesh=split, in_specs=(rows, P(), P("virt", None)), out_specs=rows, check_vma=False
    )
```

```python
import functools

import jax
import jax.numpy as jnp
from jax import lax
from jax.experimental import pallas as pl
from jax.experimental.pallas import tpu as pltpu
from jax.sharding import Mesh, PartitionSpec as P

TILE = 128
IRREPS = 4
TILES = 128
SECT = 48
OWNED = 8
VIRT = 16
ROWS = 8
EXTRA = 5
SLOTS = SECT + EXTRA
SIDE = 4
OUT_SLOTS = OWNED + 2 * SIDE
MAIN = 8
HALF, PLACE = 32, 33


def clip_count(first, count, w):
    low, high = jnp.maximum(first, w * OWNED), jnp.minimum(first + count, w * OWNED + OWNED)
    return jnp.maximum(high - low, 0)


def plan_kernel(irreps_ref, table_ref):
    def count(at, counts):
        irrep = irreps_ref[at]
        return tuple(counts[g] + (irrep == g).astype(jnp.int32) for g in range(IRREPS))

    counts = lax.fori_loop(0, TILES, count, (jnp.int32(0),) * IRREPS)
    first = jnp.int32(0)
    firsts = []
    for g in range(IRREPS):
        firsts.append(first)
        table_ref[g] = first
        table_ref[IRREPS + g] = counts[g]
        first = first + counts[g]
    for w in range(VIRT):
        best, main = clip_count(firsts[0], counts[0], w), jnp.int32(0)
        for g in range(1, IRREPS):
            held = clip_count(firsts[g], counts[g], w)
            main = jnp.where(held > best, g, main)
            best = jnp.maximum(held, best)
        table_ref[MAIN + w] = main


def plan(tile_irreps):
    return pl.pallas_call(
        plan_kernel,
        out_shape=jax.ShapeDtypeStruct((32,), jnp.int32),
        in_specs=[pl.BlockSpec(memory_space=pltpu.SMEM)],
        out_specs=pl.BlockSpec(memory_space=pltpu.SMEM),
        name="plan",
    )(tile_irreps)


def position(table_ref, w):
    main = table_ref[MAIN + w]
    first, count = table_ref[main], table_ref[IRREPS + main]
    before = jnp.maximum(first - w * OWNED, 0)
    return main, first, count, before, clip_count(first, count, w)


def pack_kernel(table_ref, own_ref, partner_ref, out_ref, tau_ref):
    for tile in range(TILES):
        columns = pl.ds(tile * TILE, TILE)
        mine = own_ref[:, columns].astype(jnp.float32)
        other = partner_ref[:, columns].astype(jnp.float32)
        tau_ref[tile] = (0.5 * (mine - other)).astype(jnp.bfloat16)
    tau_ref[TILES] = jnp.zeros((ROWS, TILE), jnp.bfloat16)

    @pl.loop(0, VIRT)
    def _(w):
        _, first, count, before, held = position(table_ref, w)
        for slot in range(SECT):
            out_ref[w, slot] = tau_ref[jnp.where(slot < count, first + slot, TILES)]
        for extra in range(EXTRA):
            at = jnp.where(extra < before, extra, extra + held)
            at = jnp.where(at < OWNED, w * OWNED + at, TILES)
            out_ref[w, SECT + extra] = tau_ref[at]


def pack(table, own, partner):
    return pl.pallas_call(
        pack_kernel,
        out_shape=jax.ShapeDtypeStruct((VIRT, SLOTS, ROWS, TILE), jnp.bfloat16),
        in_specs=[pl.BlockSpec(memory_space=pltpu.SMEM)] + [pl.BlockSpec(memory_space=pltpu.VMEM)] * 2,
        out_specs=pl.BlockSpec(memory_space=pltpu.VMEM),
        scratch_shapes=[pltpu.VMEM((TILES + 1, ROWS, TILE), jnp.bfloat16)],
        compiler_params=pltpu.CompilerParams(vmem_limit_bytes=16 << 20),
        name="pack",
    )(table, own, partner)


GROUP = 2
NT = (((1,), (1,)), ((), ()))
NN = (((1,), (0,)), ((), ()))


def tile_at(index, count=1):
    return pl.ds(pl.multiple_of(index * TILE, TILE), count * TILE)


def right_start(first, last_block):
    return jnp.minimum(last_block * OWNED - first, SECT - SIDE)


def ladder_kernel(table_ref, irreps_ref, tau_ref, block_ref, out_ref, held_ref, some_ref, part_ref):
    half, w = table_ref[HALF], table_ref[PLACE]
    main, main_first, _, before, held = position(table_ref, w)
    sign = jnp.where(half == 1, -1.0, 1.0)

    for slot in range(SLOTS):
        for src in range(0, VIRT, 2):
            rows = jnp.concatenate([tau_ref[src, slot], tau_ref[src + 1, slot]], axis=0)
            held_ref[pl.ds(src * ROWS, 2 * ROWS), pl.ds(slot * TILE, TILE)] = rows

    def tau_of(tile):
        inside = w * OWNED + tile - main_first
        outside = SECT + jnp.where(tile < before, tile, tile - held)
        return held_ref[:, tile_at(jnp.where(irreps_ref[w * OWNED + tile] == main, inside, outside))]

    def send(slot, values):
        upper = (values * sign).astype(jnp.bfloat16)
        for dest in range(VIRT):
            rows = upper[dest * ROWS : (dest + 1) * ROWS]
            out_ref[dest, slot] = rows
            out_ref[VIRT + dest, slot] = -rows

    for start in range(0, OWNED, GROUP):
        sums = lax.dot_general(
            block_ref[start * TILE : (start + GROUP) * TILE],
            held_ref[:, : SECT * TILE],
            NT,
            preferred_element_type=jnp.float32,
        )
        for tile in range(GROUP):
            send(start + tile, sums[tile * TILE : (tile + 1) * TILE].T)

    @pl.when(held < OWNED)
    def _():
        @pl.loop(0, IRREPS)
        def _(irrep):
            first, count = table_ref[irrep], table_ref[IRREPS + irrep]
            low = jnp.maximum(first - w * OWNED, 0)
            size = clip_count(first, count, w)

            @pl.when((irrep != main) & (size > 0))
            def _():
                column = w * OWNED + low - first
                start = jnp.minimum(column, SECT - SIDE)
                row = jnp.minimum(low, OWNED - SIDE)
                some_ref[...] = jnp.zeros_like(some_ref)

                @pl.loop(0, size)
                def _(at):
                    some_ref[:, tile_at(column - start + at)] = tau_of(low + at)

                part_ref[...] = lax.dot_general(
                    some_ref[:, : SIDE * TILE],
                    block_ref[tile_at(row, SIDE), tile_at(start, SIDE)],
                    NT,
                    preferred_element_type=jnp.float32,
                )

                @pl.loop(0, size)
                def _(at):
                    send(low + at, part_ref[:, tile_at(low - row + at)])

    def side(slot, edge, is_left):
        irrep = irreps_ref[w * OWNED + edge]
        first, count = table_ref[irrep], table_ref[IRREPS + irrep]
        block = (first if is_left else first + count - 1) // OWNED

        @pl.when((block != w) & (table_ref[MAIN + block] != irrep))
        def _():
            for tile in range(OWNED):
                inside = irreps_ref[w * OWNED + tile] == irrep

                @pl.when(inside)
                def _():
                    some_ref[:, tile * TILE : (tile + 1) * TILE] = tau_of(tile)

                @pl.when(jnp.logical_not(inside))
                def _():
                    some_ref[:, tile * TILE : (tile + 1) * TILE] = jnp.zeros((VIRT * ROWS, TILE), jnp.bfloat16)

            at = 0 if is_left else right_start(first, block)
            part_ref[...] = lax.dot_general(
                some_ref[...], block_ref[:, tile_at(at, SIDE)], NN, preferred_element_type=jnp.float32
            )
            for tile in range(SIDE):
                send(slot + tile, part_ref[:, tile * TILE : (tile + 1) * TILE])

    side(OWNED, 0, True)
    side(OWNED + SIDE, OWNED - 1, False)


def ladder(table, tile_irreps, taken, blocks):
    rows = VIRT * ROWS
    return pl.pallas_call(
        ladder_kernel,
        out_shape=jax.ShapeDtypeStruct((2 * VIRT, OUT_SLOTS, ROWS, TILE), jnp.bfloat16),
        in_specs=[pl.BlockSpec(memory_space=pltpu.SMEM)] * 2 + [pl.BlockSpec(memory_space=pltpu.VMEM)] * 2,
        out_specs=pl.BlockSpec(memory_space=pltpu.VMEM),
        scratch_shapes=[
            pltpu.VMEM((rows, SLOTS * TILE), jnp.bfloat16),
            pltpu.VMEM((rows, OWNED * TILE), jnp.bfloat16),
            pltpu.VMEM((rows, SIDE * TILE), jnp.float32),
        ],
        compiler_params=pltpu.CompilerParams(vmem_limit_bytes=40 << 20),
        cost_estimate=pl.CostEstimate(
            flops=2 * rows * SECT * TILE * OWNED * TILE, bytes_accessed=16 << 20, transcendentals=0
        ),
        name="ladder",
    )(table, tile_irreps, taken, blocks)


def collect_kernel(table_ref, irreps_ref, taken_ref, out_ref):
    @pl.loop(0, VIRT)
    def _(w):
        for tile in range(OWNED):
            both = [taken_ref[half * VIRT + w, tile] for half in range(2)]
            out_ref[:, tile_at(w * OWNED + tile)] = jnp.concatenate(both, axis=0)
        main, _, _, _, held = position(table_ref, w)

        @pl.when(held < OWNED)
        def _():
            @pl.loop(0, OWNED)
            def _(tile):
                at = w * OWNED + tile
                irrep = irreps_ref[at]

                @pl.when(irrep != main)
                def _():
                    first = table_ref[irrep]
                    left_block = first // OWNED
                    right_block = (first + table_ref[IRREPS + irrep] - 1) // OWNED
                    on_left = w == left_block
                    low = jnp.where(on_left, left_block + 1, left_block)
                    high = jnp.where(on_left, right_block + 1, right_block)
                    slot = jnp.where(
                        on_left,
                        OWNED + at - first,
                        OWNED + SIDE + at - first - right_start(first, right_block),
                    )
                    both = []
                    for half in range(2):
                        total = lax.fori_loop(
                            low,
                            high,
                            lambda v, total: total + taken_ref[half * VIRT + v, slot].astype(jnp.float32),
                            taken_ref[half * VIRT + w, tile].astype(jnp.float32),
                        )
                        both.append(total.astype(jnp.bfloat16))
                    out_ref[:, tile_at(at)] = jnp.concatenate(both, axis=0)


def collect(table, tile_irreps, taken):
    return pl.pallas_call(
        collect_kernel,
        out_shape=jax.ShapeDtypeStruct((2 * ROWS, TILES * TILE), jnp.bfloat16),
        in_specs=[pl.BlockSpec(memory_space=pltpu.SMEM)] * 2 + [pl.BlockSpec(memory_space=pltpu.VMEM)],
        out_specs=pl.BlockSpec(memory_space=pltpu.VMEM),
        compiler_params=pltpu.CompilerParams(vmem_limit_bytes=16 << 20),
        name="collect",
    )(table, tile_irreps, taken)


def on_device(amplitudes, tile_irreps, ladder_blocks):
    half = lax.axis_index("half")
    sent = lax.dynamic_slice_in_dim(amplitudes, (1 - half) * ROWS, ROWS, 0)
    own = lax.dynamic_slice_in_dim(amplitudes, half * ROWS, ROWS, 0)
    partner = lax.ppermute(sent, "half", [(0, 1), (1, 0)])
    place = jnp.stack([half, lax.axis_index("virt")]).astype(jnp.int32)
    table = jnp.concatenate([plan(tile_irreps), place])
    packed = pack(table, own, partner)
    taken = lax.all_to_all(packed, "virt", split_axis=0, concat_axis=0, tiled=True)
    sums = ladder(table, tile_irreps, taken, ladder_blocks)
    taken = lax.all_to_all(sums, ("half", "virt"), split_axis=0, concat_axis=0, tiled=True)
    return collect(table, tile_irreps, taken)


def solution(mesh):
    pairs, virt = mesh.devices.shape
    split = Mesh(mesh.devices.reshape(2, pairs // 2, virt), ("half", "quarter", "virt"))
    rows = P(("half", "quarter", "virt"), None)
    return jax.shard_map(
        on_device, mesh=split, in_specs=(rows, P(), P("virt", None)), out_specs=rows, check_vma=False
    )
```

```python
import functools

import jax
import jax.numpy as jnp
from jax import lax
from jax.experimental import pallas as pl
from jax.experimental.pallas import tpu as pltpu
from jax.sharding import Mesh, PartitionSpec as P

TILE = 128
IRREPS = 4
TILES = 128
SECT = 48
OWNED = 8
VIRT = 16
ROWS = 8
EXTRA = 5
SLOTS = SECT + EXTRA
SIDE = 4
OUT_SLOTS = OWNED + 2 * SIDE
MAIN = 8
HALF, PLACE = 32, 33


def clip_count(first, count, w):
    low, high = jnp.maximum(first, w * OWNED), jnp.minimum(first + count, w * OWNED + OWNED)
    return jnp.maximum(high - low, 0)


def plan_kernel(irreps_ref, blocks_ref, table_ref, near_ref, copied):
    copy = pltpu.make_async_copy(blocks_ref, near_ref, copied)
    copy.start()

    def count(at, counts):
        irrep = irreps_ref[at]
        return tuple(counts[g] + (irrep == g).astype(jnp.int32) for g in range(IRREPS))

    counts = lax.fori_loop(0, TILES, count, (jnp.int32(0),) * IRREPS)
    first = jnp.int32(0)
    firsts = []
    for g in range(IRREPS):
        firsts.append(first)
        table_ref[g] = first
        table_ref[IRREPS + g] = counts[g]
        first = first + counts[g]
    for w in range(VIRT):
        best, main = clip_count(firsts[0], counts[0], w), jnp.int32(0)
        for g in range(1, IRREPS):
            held = clip_count(firsts[g], counts[g], w)
            main = jnp.where(held > best, g, main)
            best = jnp.maximum(held, best)
        table_ref[MAIN + w] = main
    copy.wait()


def plan(tile_irreps, blocks):
    return pl.pallas_call(
        plan_kernel,
        out_shape=(jax.ShapeDtypeStruct((32,), jnp.int32), jax.ShapeDtypeStruct(blocks.shape, blocks.dtype)),
        in_specs=[pl.BlockSpec(memory_space=pltpu.SMEM), pl.BlockSpec(memory_space=pltpu.HBM)],
        out_specs=(pl.BlockSpec(memory_space=pltpu.SMEM), pl.BlockSpec(memory_space=pltpu.VMEM)),
        scratch_shapes=[pltpu.SemaphoreType.DMA],
        compiler_params=pltpu.CompilerParams(vmem_limit_bytes=37 << 20),
        cost_estimate=pl.CostEstimate(flops=0, bytes_accessed=2 * blocks.size * 2, transcendentals=0),
        name="plan",
    )(tile_irreps, blocks)


def position(table_ref, w):
    main = table_ref[MAIN + w]
    first, count = table_ref[main], table_ref[IRREPS + main]
    before = jnp.maximum(first - w * OWNED, 0)
    return main, first, count, before, clip_count(first, count, w)


def pack_kernel(table_ref, own_ref, partner_ref, out_ref, tau_ref):
    for tile in range(TILES):
        columns = pl.ds(tile * TILE, TILE)
        mine = own_ref[:, columns].astype(jnp.float32)
        other = partner_ref[:, columns].astype(jnp.float32)
        tau_ref[tile] = (0.5 * (mine - other)).astype(jnp.bfloat16)
    tau_ref[TILES] = jnp.zeros((ROWS, TILE), jnp.bfloat16)

    @pl.loop(0, VIRT)
    def _(w):
        _, first, count, before, held = position(table_ref, w)
        for slot in range(SECT):
            out_ref[w, slot] = tau_ref[jnp.where(slot < count, first + slot, TILES)]
        for extra in range(EXTRA):
            at = jnp.where(extra < before, extra, extra + held)
            at = jnp.where(at < OWNED, w * OWNED + at, TILES)
            out_ref[w, SECT + extra] = tau_ref[at]


def pack(table, own, partner):
    return pl.pallas_call(
        pack_kernel,
        out_shape=jax.ShapeDtypeStruct((VIRT, SLOTS, ROWS, TILE), jnp.bfloat16),
        in_specs=[pl.BlockSpec(memory_space=pltpu.SMEM)] + [pl.BlockSpec(memory_space=pltpu.VMEM)] * 2,
        out_specs=pl.BlockSpec(memory_space=pltpu.VMEM),
        scratch_shapes=[pltpu.VMEM((TILES + 1, ROWS, TILE), jnp.bfloat16)],
        compiler_params=pltpu.CompilerParams(vmem_limit_bytes=16 << 20),
        name="pack",
    )(table, own, partner)


GROUP = 2
NT = (((1,), (1,)), ((), ()))
NN = (((1,), (0,)), ((), ()))


def tile_at(index, count=1):
    return pl.ds(pl.multiple_of(index * TILE, TILE), count * TILE)


def right_start(first, last_block):
    return jnp.minimum(last_block * OWNED - first, SECT - SIDE)


def ladder_kernel(table_ref, irreps_ref, tau_ref, block_ref, out_ref, held_ref, some_ref, part_ref):
    half, w = table_ref[HALF], table_ref[PLACE]
    main, main_first, _, before, held = position(table_ref, w)
    sign = jnp.where(half == 1, -1.0, 1.0)

    for slot in range(SLOTS):
        for src in range(0, VIRT, 2):
            rows = jnp.concatenate([tau_ref[src, slot], tau_ref[src + 1, slot]], axis=0)
            held_ref[pl.ds(src * ROWS, 2 * ROWS), pl.ds(slot * TILE, TILE)] = rows

    def tau_of(tile):
        inside = w * OWNED + tile - main_first
        outside = SECT + jnp.where(tile < before, tile, tile - held)
        return held_ref[:, tile_at(jnp.where(irreps_ref[w * OWNED + tile] == main, inside, outside))]

    def send(slot, values):
        upper = (values * sign).astype(jnp.bfloat16)
        for dest in range(VIRT):
            rows = upper[dest * ROWS : (dest + 1) * ROWS]
            out_ref[dest, slot] = rows
            out_ref[VIRT + dest, slot] = -rows

    for start in range(0, OWNED, GROUP):
        sums = lax.dot_general(
            block_ref[start * TILE : (start + GROUP) * TILE],
            held_ref[:, : SECT * TILE],
            NT,
            preferred_element_type=jnp.float32,
        )
        for tile in range(GROUP):
            send(start + tile, sums[tile * TILE : (tile + 1) * TILE].T)

    @pl.when(held < OWNED)
    def _():
        @pl.loop(0, IRREPS)
        def _(irrep):
            first, count = table_ref[irrep], table_ref[IRREPS + irrep]
            low = jnp.maximum(first - w * OWNED, 0)
            size = clip_count(first, count, w)

            @pl.when((irrep != main) & (size > 0))
            def _():
                column = w * OWNED + low - first
                start = jnp.minimum(column, SECT - SIDE)
                row = jnp.minimum(low, OWNED - SIDE)
                some_ref[...] = jnp.zeros_like(some_ref)

                @pl.loop(0, size)
                def _(at):
                    some_ref[:, tile_at(column - start + at)] = tau_of(low + at)

                part_ref[...] = lax.dot_general(
                    some_ref[:, : SIDE * TILE],
                    block_ref[tile_at(row, SIDE), tile_at(start, SIDE)],
                    NT,
                    preferred_element_type=jnp.float32,
                )

                @pl.loop(0, size)
                def _(at):
                    send(low + at, part_ref[:, tile_at(low - row + at)])

    def side(slot, edge, is_left):
        irrep = irreps_ref[w * OWNED + edge]
        first, count = table_ref[irrep], table_ref[IRREPS + irrep]
        block = (first if is_left else first + count - 1) // OWNED

        @pl.when((block != w) & (table_ref[MAIN + block] != irrep))
        def _():
            for tile in range(OWNED):
                inside = irreps_ref[w * OWNED + tile] == irrep

                @pl.when(inside)
                def _():
                    some_ref[:, tile * TILE : (tile + 1) * TILE] = tau_of(tile)

                @pl.when(jnp.logical_not(inside))
                def _():
                    some_ref[:, tile * TILE : (tile + 1) * TILE] = jnp.zeros((VIRT * ROWS, TILE), jnp.bfloat16)

            at = 0 if is_left else right_start(first, block)
            part_ref[...] = lax.dot_general(
                some_ref[...], block_ref[:, tile_at(at, SIDE)], NN, preferred_element_type=jnp.float32
            )
            for tile in range(SIDE):
                send(slot + tile, part_ref[:, tile * TILE : (tile + 1) * TILE])

    side(OWNED, 0, True)
    side(OWNED + SIDE, OWNED - 1, False)


def ladder(table, tile_irreps, taken, blocks):
    rows = VIRT * ROWS
    return pl.pallas_call(
        ladder_kernel,
        out_shape=jax.ShapeDtypeStruct((2 * VIRT, OUT_SLOTS, ROWS, TILE), jnp.bfloat16),
        in_specs=[pl.BlockSpec(memory_space=pltpu.SMEM)] * 2 + [pl.BlockSpec(memory_space=pltpu.VMEM)] * 2,
        out_specs=pl.BlockSpec(memory_space=pltpu.VMEM),
        scratch_shapes=[
            pltpu.VMEM((rows, SLOTS * TILE), jnp.bfloat16),
            pltpu.VMEM((rows, OWNED * TILE), jnp.bfloat16),
            pltpu.VMEM((rows, SIDE * TILE), jnp.float32),
        ],
        compiler_params=pltpu.CompilerParams(vmem_limit_bytes=24 << 20),
        cost_estimate=pl.CostEstimate(
            flops=2 * rows * SECT * TILE * OWNED * TILE, bytes_accessed=16 << 20, transcendentals=0
        ),
        name="ladder",
    )(table, tile_irreps, taken, blocks)


def collect_kernel(table_ref, irreps_ref, taken_ref, out_ref):
    @pl.loop(0, VIRT)
    def _(w):
        for tile in range(OWNED):
            both = [taken_ref[half * VIRT + w, tile] for half in range(2)]
            out_ref[:, tile_at(w * OWNED + tile)] = jnp.concatenate(both, axis=0)
        main, _, _, _, held = position(table_ref, w)

        @pl.when(held < OWNED)
        def _():
            @pl.loop(0, OWNED)
            def _(tile):
                at = w * OWNED + tile
                irrep = irreps_ref[at]

                @pl.when(irrep != main)
                def _():
                    first = table_ref[irrep]
                    left_block = first // OWNED
                    right_block = (first + table_ref[IRREPS + irrep] - 1) // OWNED
                    on_left = w == left_block
                    low = jnp.where(on_left, left_block + 1, left_block)
                    high = jnp.where(on_left, right_block + 1, right_block)
                    slot = jnp.where(
                        on_left,
                        OWNED + at - first,
                        OWNED + SIDE + at - first - right_start(first, right_block),
                    )
                    both = []
                    for half in range(2):
                        total = lax.fori_loop(
                            low,
                            high,
                            lambda v, total: total + taken_ref[half * VIRT + v, slot].astype(jnp.float32),
                            taken_ref[half * VIRT + w, tile].astype(jnp.float32),
                        )
                        both.append(total.astype(jnp.bfloat16))
                    out_ref[:, tile_at(at)] = jnp.concatenate(both, axis=0)


def collect(table, tile_irreps, taken):
    return pl.pallas_call(
        collect_kernel,
        out_shape=jax.ShapeDtypeStruct((2 * ROWS, TILES * TILE), jnp.bfloat16),
        in_specs=[pl.BlockSpec(memory_space=pltpu.SMEM)] * 2 + [pl.BlockSpec(memory_space=pltpu.VMEM)],
        out_specs=pl.BlockSpec(memory_space=pltpu.VMEM),
        compiler_params=pltpu.CompilerParams(vmem_limit_bytes=16 << 20),
        name="collect",
    )(table, tile_irreps, taken)


def on_device(amplitudes, tile_irreps, ladder_blocks):
    half = lax.axis_index("half")
    sent = lax.dynamic_slice_in_dim(amplitudes, (1 - half) * ROWS, ROWS, 0)
    own = lax.dynamic_slice_in_dim(amplitudes, half * ROWS, ROWS, 0)
    partner = lax.ppermute(sent, "half", [(0, 1), (1, 0)])
    place = jnp.stack([half, lax.axis_index("virt")]).astype(jnp.int32)
    table, near = plan(tile_irreps, ladder_blocks)
    table = jnp.concatenate([table, place])
    packed = pack(table, own, partner)
    taken = lax.all_to_all(packed, "virt", split_axis=0, concat_axis=0, tiled=True)
    sums = ladder(table, tile_irreps, taken, near)
    taken = lax.all_to_all(sums, ("half", "virt"), split_axis=0, concat_axis=0, tiled=True)
    return collect(table, tile_irreps, taken)


def solution(mesh):
    pairs, virt = mesh.devices.shape
    split = Mesh(mesh.devices.reshape(2, pairs // 2, virt), ("half", "quarter", "virt"))
    rows = P(("half", "quarter", "virt"), None)
    return jax.shard_map(
        on_device, mesh=split, in_specs=(rows, P(), P("virt", None)), out_specs=rows, check_vma=False
    )
```

```python
import functools

import jax
import jax.numpy as jnp
from jax import lax
from jax.experimental import pallas as pl
from jax.experimental.pallas import tpu as pltpu
from jax.sharding import Mesh, PartitionSpec as P

TILE = 128
IRREPS = 4
TILES = 128
SECT = 48
OWNED = 8
VIRT = 16
ROWS = 8
EXTRA = 5
SLOTS = SECT + EXTRA
SIDE = 4
OUT_SLOTS = OWNED + 2 * SIDE
MAIN = 8
HALF, PLACE = 32, 33


def clip_count(first, count, w):
    low, high = jnp.maximum(first, w * OWNED), jnp.minimum(first + count, w * OWNED + OWNED)
    return jnp.maximum(high - low, 0)


def plan_kernel(irreps_ref, blocks_ref, table_ref, near_ref, copied):
    copy = pltpu.make_async_copy(blocks_ref, near_ref, copied)
    copy.start()

    def count(at, counts):
        irrep = irreps_ref[at]
        return tuple(counts[g] + (irrep == g).astype(jnp.int32) for g in range(IRREPS))

    counts = lax.fori_loop(0, TILES, count, (jnp.int32(0),) * IRREPS)
    first = jnp.int32(0)
    firsts = []
    for g in range(IRREPS):
        firsts.append(first)
        table_ref[g] = first
        table_ref[IRREPS + g] = counts[g]
        first = first + counts[g]
    for w in range(VIRT):
        best, main = clip_count(firsts[0], counts[0], w), jnp.int32(0)
        for g in range(1, IRREPS):
            held = clip_count(firsts[g], counts[g], w)
            main = jnp.where(held > best, g, main)
            best = jnp.maximum(held, best)
        table_ref[MAIN + w] = main
    copy.wait()


def plan(tile_irreps, blocks):
    return pl.pallas_call(
        plan_kernel,
        out_shape=(jax.ShapeDtypeStruct((32,), jnp.int32), jax.ShapeDtypeStruct(blocks.shape, blocks.dtype)),
        in_specs=[pl.BlockSpec(memory_space=pltpu.SMEM), pl.BlockSpec(memory_space=pltpu.HBM)],
        out_specs=(pl.BlockSpec(memory_space=pltpu.SMEM), pl.BlockSpec(memory_space=pltpu.VMEM)),
        scratch_shapes=[pltpu.SemaphoreType.DMA],
        compiler_params=pltpu.CompilerParams(vmem_limit_bytes=37 << 20),
        cost_estimate=pl.CostEstimate(flops=0, bytes_accessed=2 * blocks.size * 2, transcendentals=0),
        name="plan",
    )(tile_irreps, blocks)


def position(table_ref, w):
    main = table_ref[MAIN + w]
    first, count = table_ref[main], table_ref[IRREPS + main]
    before = jnp.maximum(first - w * OWNED, 0)
    return main, first, count, before, clip_count(first, count, w)


def pack_kernel(table_ref, own_ref, partner_ref, out_ref, tau_ref):
    for tile in range(TILES):
        columns = pl.ds(tile * TILE, TILE)
        mine = own_ref[:, columns].astype(jnp.float32)
        other = partner_ref[:, columns].astype(jnp.float32)
        tau_ref[tile] = (0.5 * (mine - other)).astype(jnp.bfloat16)
    tau_ref[TILES:] = jnp.zeros((SECT, ROWS, TILE), jnp.bfloat16)

    @pl.loop(0, VIRT)
    def _(w):
        _, first, _, before, held = position(table_ref, w)
        out_ref[w, :SECT] = tau_ref[pl.ds(first, SECT)]
        for extra in range(EXTRA):
            at = jnp.where(extra < before, extra, extra + held)
            at = jnp.where(at < OWNED, w * OWNED + at, TILES)
            out_ref[w, SECT + extra] = tau_ref[at]


def pack(table, own, partner):
    return pl.pallas_call(
        pack_kernel,
        out_shape=jax.ShapeDtypeStruct((VIRT, SLOTS, ROWS, TILE), jnp.bfloat16),
        in_specs=[pl.BlockSpec(memory_space=pltpu.SMEM)] + [pl.BlockSpec(memory_space=pltpu.VMEM)] * 2,
        out_specs=pl.BlockSpec(memory_space=pltpu.VMEM),
        scratch_shapes=[pltpu.VMEM((TILES + SECT, ROWS, TILE), jnp.bfloat16)],
        compiler_params=pltpu.CompilerParams(vmem_limit_bytes=16 << 20),
        name="pack",
    )(table, own, partner)


GROUP = 2
SHORT = 32
NT = (((1,), (1,)), ((), ()))
NN = (((1,), (0,)), ((), ()))


def tile_at(index, count=1):
    start = index * TILE if isinstance(index, int) else pl.multiple_of(index * TILE, TILE)
    return pl.ds(start, count * TILE)


def right_start(first, last_block):
    return jnp.minimum(last_block * OWNED - first, SECT - SIDE)


def ladder_kernel(table_ref, irreps_ref, tau_ref, block_ref, out_ref, held_ref, some_ref, part_ref):
    half, w = table_ref[HALF], table_ref[PLACE]
    main, main_first, main_count, before, held = position(table_ref, w)
    sign = jnp.where(half == 1, -1.0, 1.0)

    for slot in range(SLOTS):
        for src in range(0, VIRT, 2):
            rows = jnp.concatenate([tau_ref[src, slot], tau_ref[src + 1, slot]], axis=0)
            held_ref[pl.ds(src * ROWS, 2 * ROWS), pl.ds(slot * TILE, TILE)] = rows

    def tau_of(tile):
        inside = w * OWNED + tile - main_first
        outside = SECT + jnp.where(tile < before, tile, tile - held)
        return held_ref[:, tile_at(jnp.where(irreps_ref[w * OWNED + tile] == main, inside, outside))]

    def send(slot, values):
        upper = (values * sign).astype(jnp.bfloat16)
        for dest in range(VIRT):
            rows = upper[dest * ROWS : (dest + 1) * ROWS]
            out_ref[dest, :, tile_at(slot)] = rows
            out_ref[VIRT + dest, :, tile_at(slot)] = -rows

    def multiply(depth):
        @pl.loop(main_count, depth)
        def _(slot):
            held_ref[:, tile_at(slot)] = jnp.zeros((VIRT * ROWS, TILE), jnp.bfloat16)

        for start in range(0, OWNED, GROUP):
            sums = lax.dot_general(
                block_ref[start * TILE : (start + GROUP) * TILE, : depth * TILE],
                held_ref[:, : depth * TILE],
                NT,
                preferred_element_type=jnp.float32,
            )
            for tile in range(GROUP):
                send(start + tile, sums[tile * TILE : (tile + 1) * TILE].T)

    pl.when(main_count <= SHORT)(lambda: multiply(SHORT))
    pl.when(main_count > SHORT)(lambda: multiply(SECT))

    @pl.when(held < OWNED)
    def _():
        @pl.loop(0, IRREPS)
        def _(irrep):
            first, count = table_ref[irrep], table_ref[IRREPS + irrep]
            low = jnp.maximum(first - w * OWNED, 0)
            size = clip_count(first, count, w)

            @pl.when((irrep != main) & (size > 0))
            def _():
                column = w * OWNED + low - first
                start = jnp.minimum(column, SECT - SIDE)
                row = jnp.minimum(low, OWNED - SIDE)
                some_ref[...] = jnp.zeros_like(some_ref)

                @pl.loop(0, size)
                def _(at):
                    some_ref[:, tile_at(column - start + at)] = tau_of(low + at)

                part_ref[...] = lax.dot_general(
                    some_ref[:, : SIDE * TILE],
                    block_ref[tile_at(row, SIDE), tile_at(start, SIDE)],
                    NT,
                    preferred_element_type=jnp.float32,
                )

                @pl.loop(0, size)
                def _(at):
                    send(low + at, part_ref[:, tile_at(low - row + at)])

    def side(slot, edge, is_left):
        irrep = irreps_ref[w * OWNED + edge]
        first, count = table_ref[irrep], table_ref[IRREPS + irrep]
        block = (first if is_left else first + count - 1) // OWNED

        @pl.when((block != w) & (table_ref[MAIN + block] != irrep))
        def _():
            for tile in range(OWNED):
                inside = irreps_ref[w * OWNED + tile] == irrep

                @pl.when(inside)
                def _():
                    some_ref[:, tile * TILE : (tile + 1) * TILE] = tau_of(tile)

                @pl.when(jnp.logical_not(inside))
                def _():
                    some_ref[:, tile * TILE : (tile + 1) * TILE] = jnp.zeros((VIRT * ROWS, TILE), jnp.bfloat16)

            at = 0 if is_left else right_start(first, block)
            part_ref[...] = lax.dot_general(
                some_ref[...], block_ref[:, tile_at(at, SIDE)], NN, preferred_element_type=jnp.float32
            )
            for tile in range(SIDE):
                send(slot + tile, part_ref[:, tile * TILE : (tile + 1) * TILE])

    side(OWNED, 0, True)
    side(OWNED + SIDE, OWNED - 1, False)


def ladder(table, tile_irreps, taken, blocks):
    rows = VIRT * ROWS
    return pl.pallas_call(
        ladder_kernel,
        out_shape=jax.ShapeDtypeStruct((2 * VIRT, ROWS, OUT_SLOTS * TILE), jnp.bfloat16),
        in_specs=[pl.BlockSpec(memory_space=pltpu.SMEM)] * 2 + [pl.BlockSpec(memory_space=pltpu.VMEM)] * 2,
        out_specs=pl.BlockSpec(memory_space=pltpu.VMEM),
        scratch_shapes=[
            pltpu.VMEM((rows, SLOTS * TILE), jnp.bfloat16),
            pltpu.VMEM((rows, OWNED * TILE), jnp.bfloat16),
            pltpu.VMEM((rows, SIDE * TILE), jnp.float32),
        ],
        compiler_params=pltpu.CompilerParams(vmem_limit_bytes=24 << 20),
        cost_estimate=pl.CostEstimate(
            flops=2 * rows * SECT * TILE * OWNED * TILE, bytes_accessed=16 << 20, transcendentals=0
        ),
        name="ladder",
    )(table, tile_irreps, taken, blocks)


def collect_kernel(table_ref, taken_ref, out_ref, mixed_ref, total_ref, sent, mixed_sent):
    def copy(w, half):
        return pltpu.make_async_copy(
            taken_ref.at[half * VIRT + w, :, : OWNED * TILE], out_ref.at[half, :, tile_at(w * OWNED, OWNED)], sent
        )

    def mixed_copy(w, half):
        return pltpu.make_async_copy(
            mixed_ref.at[half * VIRT + w], out_ref.at[half, :, tile_at(w * OWNED, OWNED)], mixed_sent
        )

    def is_mixed(w):
        return position(table_ref, w)[4] < OWNED

    @pl.loop(0, VIRT)
    def _(w):
        mixed = is_mixed(w)

        @pl.when(jnp.logical_not(mixed))
        def _():
            for half in range(2):
                copy(w, half).start()

    @pl.loop(0, VIRT)
    def _(w):
        @pl.when(is_mixed(w))
        def _():
            main = table_ref[MAIN + w]
            for half in range(2):
                mixed_ref[half * VIRT + w] = taken_ref[half * VIRT + w, :, : OWNED * TILE]

            @pl.loop(0, IRREPS)
            def _(irrep):
                first, count = table_ref[irrep], table_ref[IRREPS + irrep]
                size = clip_count(first, count, w)

                @pl.when((irrep != main) & (size > 0))
                def _():
                    left_block, right_block = first // OWNED, (first + count - 1) // OWNED
                    on_left = w == left_block
                    low = jnp.where(on_left, left_block + 1, left_block)
                    high = jnp.where(on_left, right_block + 1, right_block)
                    tile = jnp.maximum(first - w * OWNED, 0)
                    offset = jnp.where(on_left, 0, w * OWNED - first - right_start(first, right_block))
                    slots = tile_at(jnp.where(on_left, OWNED, OWNED + SIDE), SIDE)

                    def add(v, totals):
                        return tuple(
                            totals[half] + taken_ref[half * VIRT + v, :, slots].astype(jnp.float32) for half in range(2)
                        )

                    zeros = jnp.zeros((ROWS, SIDE * TILE), jnp.float32)
                    totals = lax.fori_loop(low, high, add, (zeros, zeros))
                    for half in range(2):
                        total_ref[half] = totals[half]

                    @pl.loop(0, size)
                    def _(at):
                        columns = tile_at(tile + at)
                        for half in range(2):
                            own = taken_ref[half * VIRT + w, :, columns].astype(jnp.float32)
                            total = own + total_ref[half, :, tile_at(offset + at)]
                            mixed_ref[half * VIRT + w, :, columns] = total.astype(jnp.bfloat16)

            for half in range(2):
                mixed_copy(w, half).start()

    @pl.loop(0, VIRT)
    def _(w):
        mixed = is_mixed(w)

        @pl.when(mixed)
        def _():
            for half in range(2):
                mixed_copy(w, half).wait()

        @pl.when(jnp.logical_not(mixed))
        def _():
            for half in range(2):
                copy(w, half).wait()


def collect(table, taken):
    out = pl.pallas_call(
        collect_kernel,
        out_shape=jax.ShapeDtypeStruct((2, ROWS, TILES * TILE), jnp.bfloat16),
        in_specs=[pl.BlockSpec(memory_space=pltpu.SMEM), pl.BlockSpec(memory_space=pltpu.VMEM)],
        out_specs=pl.BlockSpec(memory_space=pltpu.HBM),
        scratch_shapes=[
            pltpu.VMEM((2 * VIRT, ROWS, OWNED * TILE), jnp.bfloat16),
            pltpu.VMEM((2, ROWS, SIDE * TILE), jnp.float32),
            pltpu.SemaphoreType.DMA,
            pltpu.SemaphoreType.DMA,
        ],
        compiler_params=pltpu.CompilerParams(vmem_limit_bytes=16 << 20),
        name="collect",
    )(table, taken)
    return out.reshape(2 * ROWS, TILES * TILE)


def on_device(amplitudes, tile_irreps, ladder_blocks):
    half = lax.axis_index("half")
    sent = lax.dynamic_slice_in_dim(amplitudes, (1 - half) * ROWS, ROWS, 0)
    own = lax.dynamic_slice_in_dim(amplitudes, half * ROWS, ROWS, 0)
    partner = lax.ppermute(sent, "half", [(0, 1), (1, 0)])
    place = jnp.stack([half, lax.axis_index("virt")]).astype(jnp.int32)
    table, near = plan(tile_irreps, ladder_blocks)
    table = jnp.concatenate([table, place])
    packed = pack(table, own, partner)
    taken = lax.all_to_all(packed, "virt", split_axis=0, concat_axis=0, tiled=True)
    sums = ladder(table, tile_irreps, taken, near)
    taken = lax.all_to_all(sums, ("half", "virt"), split_axis=0, concat_axis=0, tiled=True)
    return collect(table, taken)


def solution(mesh):
    pairs, virt = mesh.devices.shape
    split = Mesh(mesh.devices.reshape(2, pairs // 2, virt), ("half", "quarter", "virt"))
    rows = P(("half", "quarter", "virt"), None)
    return jax.shard_map(
        on_device, mesh=split, in_specs=(rows, P(), P("virt", None)), out_specs=rows, check_vma=False
    )
```

```python
import functools

import jax
import jax.numpy as jnp
from jax import lax
from jax.experimental import pallas as pl
from jax.experimental.pallas import tpu as pltpu
from jax.sharding import Mesh, PartitionSpec as P

TILE = 128
IRREPS = 4
TILES = 128
SECT = 48
OWNED = 8
VIRT = 16
ROWS = 8
EXTRA = 5
SLOTS = SECT + EXTRA
SIDE = 4
OUT_SLOTS = OWNED + 2 * SIDE - 1
MAIN, HELD, LEFT, HALF, PLACE = 8, 24, 40, 44, 45


def clip_count(first, count, w):
    low, high = jnp.maximum(first, w * OWNED), jnp.minimum(first + count, w * OWNED + OWNED)
    return jnp.maximum(high - low, 0)


def plan_kernel(irreps_ref, blocks_ref, table_ref, near_ref, copied):
    copy = pltpu.make_async_copy(blocks_ref, near_ref, copied)
    copy.start()

    def count(at, counts):
        irrep = irreps_ref[at]
        return tuple(counts[g] + (irrep == g).astype(jnp.int32) for g in range(IRREPS))

    counts = lax.fori_loop(0, TILES, count, (jnp.int32(0),) * IRREPS)
    first = jnp.int32(0)
    firsts = []
    for g in range(IRREPS):
        firsts.append(first)
        table_ref[g] = first
        table_ref[IRREPS + g] = counts[g]
        first = first + counts[g]
    for w in range(VIRT):
        best, main = clip_count(firsts[0], counts[0], w), jnp.int32(0)
        for g in range(1, IRREPS):
            held = clip_count(firsts[g], counts[g], w)
            main = jnp.where(held > best, g, main)
            best = jnp.maximum(held, best)
        table_ref[MAIN + w] = main
        table_ref[HELD + w] = best
    for g in range(IRREPS):
        block = jnp.minimum(firsts[g] // OWNED, VIRT - 1)
        alone = (firsts[g] + counts[g] - 1) // OWNED == block
        leaves = (table_ref[MAIN + block] != g) & (counts[g] > 0) & jnp.logical_not(alone)
        table_ref[LEFT + g] = jnp.where(leaves, (block + 1) * OWNED - firsts[g], 0)
    copy.wait()


def plan(tile_irreps, blocks):
    return pl.pallas_call(
        plan_kernel,
        out_shape=(jax.ShapeDtypeStruct((HALF,), jnp.int32), jax.ShapeDtypeStruct(blocks.shape, blocks.dtype)),
        in_specs=[pl.BlockSpec(memory_space=pltpu.SMEM), pl.BlockSpec(memory_space=pltpu.HBM)],
        out_specs=(pl.BlockSpec(memory_space=pltpu.SMEM), pl.BlockSpec(memory_space=pltpu.VMEM)),
        scratch_shapes=[pltpu.SemaphoreType.DMA],
        compiler_params=pltpu.CompilerParams(vmem_limit_bytes=37 << 20),
        cost_estimate=pl.CostEstimate(flops=0, bytes_accessed=2 * blocks.size * 2, transcendentals=0),
        name="plan",
    )(tile_irreps, blocks)


def position(table_ref, w):
    main = table_ref[MAIN + w]
    first, count = table_ref[main], table_ref[IRREPS + main]
    return main, first, count, jnp.maximum(first - w * OWNED, 0), table_ref[HELD + w]


def pack_kernel(table_ref, own_ref, partner_ref, out_ref, tau_ref):
    for tile in range(TILES):
        columns = pl.ds(tile * TILE, TILE)
        mine = own_ref[:, columns].astype(jnp.float32)
        other = partner_ref[:, columns].astype(jnp.float32)
        tau_ref[tile] = (0.5 * (mine - other)).astype(jnp.bfloat16)
    tau_ref[TILES:] = jnp.zeros((SECT, ROWS, TILE), jnp.bfloat16)

    @pl.loop(0, VIRT)
    def _(w):
        _, first, _, before, held = position(table_ref, w)
        out_ref[w, :SECT] = tau_ref[pl.ds(first, SECT)]
        for extra in range(EXTRA):
            at = jnp.where(extra < before, extra, extra + held)
            at = jnp.where(at < OWNED, w * OWNED + at, TILES)
            out_ref[w, SECT + extra] = tau_ref[at]


def pack(table, own, partner):
    return pl.pallas_call(
        pack_kernel,
        out_shape=jax.ShapeDtypeStruct((VIRT, SLOTS, ROWS, TILE), jnp.bfloat16),
        in_specs=[pl.BlockSpec(memory_space=pltpu.SMEM)] + [pl.BlockSpec(memory_space=pltpu.VMEM)] * 2,
        out_specs=pl.BlockSpec(memory_space=pltpu.VMEM),
        scratch_shapes=[pltpu.VMEM((TILES + SECT, ROWS, TILE), jnp.bfloat16)],
        compiler_params=pltpu.CompilerParams(vmem_limit_bytes=16 << 20),
        name="pack",
    )(table, own, partner)


GROUP = 2
SHORT = 32
NT = (((1,), (1,)), ((), ()))
NN = (((1,), (0,)), ((), ()))


def tile_at(index, count=1):
    start = index * TILE if isinstance(index, int) else pl.multiple_of(index * TILE, TILE)
    return pl.ds(start, count * TILE)


def right_start(first, last_block):
    return jnp.minimum(last_block * OWNED - first, SECT - SIDE)


def ladder_kernel(table_ref, irreps_ref, tau_ref, block_ref, out_ref, held_ref, some_ref, part_ref):
    half, w = table_ref[HALF], table_ref[PLACE]
    main, main_first, main_count, before, held = position(table_ref, w)
    sign = jnp.where(half == 1, -1.0, 1.0)

    for slot in range(SLOTS):
        for src in range(0, VIRT, 2):
            rows = jnp.concatenate([tau_ref[src, slot], tau_ref[src + 1, slot]], axis=0)
            held_ref[pl.ds(src * ROWS, 2 * ROWS), pl.ds(slot * TILE, TILE)] = rows

    def tau_of(tile):
        inside = w * OWNED + tile - main_first
        outside = SECT + jnp.where(tile < before, tile, tile - held)
        return held_ref[:, tile_at(jnp.where(irreps_ref[w * OWNED + tile] == main, inside, outside))]

    def send(slot, values):
        upper = (values * sign).astype(jnp.bfloat16)
        for dest in range(VIRT):
            rows = upper[dest * ROWS : (dest + 1) * ROWS]
            out_ref[dest, :, tile_at(slot)] = rows
            out_ref[VIRT + dest, :, tile_at(slot)] = -rows

    def multiply(depth):
        @pl.loop(main_count, depth)
        def _(slot):
            held_ref[:, tile_at(slot)] = jnp.zeros((VIRT * ROWS, TILE), jnp.bfloat16)

        for start in range(0, OWNED, GROUP):
            sums = lax.dot_general(
                block_ref[start * TILE : (start + GROUP) * TILE, : depth * TILE],
                held_ref[:, : depth * TILE],
                NT,
                preferred_element_type=jnp.float32,
            )
            for tile in range(GROUP):
                send(start + tile, sums[tile * TILE : (tile + 1) * TILE].T)

    pl.when(main_count <= SHORT)(lambda: multiply(SHORT))
    pl.when(main_count > SHORT)(lambda: multiply(SECT))

    @pl.when(held < OWNED)
    def _():
        @pl.loop(0, IRREPS)
        def _(irrep):
            first, count = table_ref[irrep], table_ref[IRREPS + irrep]
            low = jnp.maximum(first - w * OWNED, 0)
            size = clip_count(first, count, w)

            @pl.when((irrep != main) & (size > 0))
            def _():
                column = w * OWNED + low - first
                start = jnp.minimum(column, SECT - SIDE)
                row = jnp.minimum(low, OWNED - SIDE)
                some_ref[...] = jnp.zeros_like(some_ref)

                @pl.loop(0, size)
                def _(at):
                    some_ref[:, tile_at(column - start + at)] = tau_of(low + at)

                part_ref[...] = lax.dot_general(
                    some_ref[:, : SIDE * TILE],
                    block_ref[tile_at(row, SIDE), tile_at(start, SIDE)],
                    NT,
                    preferred_element_type=jnp.float32,
                )

                @pl.loop(0, size)
                def _(at):
                    send(low + at, part_ref[:, tile_at(low - row + at)])

    def side(edge, is_left):
        irrep = irreps_ref[w * OWNED + edge]
        first, count = table_ref[irrep], table_ref[IRREPS + irrep]
        block = (first if is_left else first + count - 1) // OWNED

        @pl.when((block != w) & (table_ref[MAIN + block] != irrep))
        def _():
            for tile in range(OWNED):
                inside = irreps_ref[w * OWNED + tile] == irrep

                @pl.when(inside)
                def _():
                    some_ref[:, tile * TILE : (tile + 1) * TILE] = tau_of(tile)

                @pl.when(jnp.logical_not(inside))
                def _():
                    some_ref[:, tile * TILE : (tile + 1) * TILE] = jnp.zeros((VIRT * ROWS, TILE), jnp.bfloat16)

            at = 0 if is_left else right_start(first, block)
            part_ref[...] = lax.dot_general(
                some_ref[...], block_ref[:, tile_at(at, SIDE)], NN, preferred_element_type=jnp.float32
            )
            low = 0 if is_left else block * OWNED - first - at
            size = table_ref[LEFT + irrep] if is_left else first + count - block * OWNED
            slot = OWNED if is_left else OWNED + table_ref[LEFT + irrep]

            @pl.loop(0, size)
            def _(tile):
                send(slot + tile, part_ref[:, tile_at(low + tile)])

    side(0, True)
    side(OWNED - 1, False)


def ladder(table, tile_irreps, taken, blocks):
    rows = VIRT * ROWS
    return pl.pallas_call(
        ladder_kernel,
        out_shape=jax.ShapeDtypeStruct((2 * VIRT, ROWS, OUT_SLOTS * TILE), jnp.bfloat16),
        in_specs=[pl.BlockSpec(memory_space=pltpu.SMEM)] * 2 + [pl.BlockSpec(memory_space=pltpu.VMEM)] * 2,
        out_specs=pl.BlockSpec(memory_space=pltpu.VMEM),
        scratch_shapes=[
            pltpu.VMEM((rows, SLOTS * TILE), jnp.bfloat16),
            pltpu.VMEM((rows, OWNED * TILE), jnp.bfloat16),
            pltpu.VMEM((rows, SIDE * TILE), jnp.float32),
        ],
        compiler_params=pltpu.CompilerParams(vmem_limit_bytes=24 << 20),
        cost_estimate=pl.CostEstimate(
            flops=2 * rows * SECT * TILE * OWNED * TILE, bytes_accessed=16 << 20, transcendentals=0
        ),
        name="ladder",
    )(table, tile_irreps, taken, blocks)


def collect_kernel(table_ref, taken_ref, out_ref, mixed_ref, total_ref, sent):
    def send(source, w):
        for half in range(2):
            pltpu.make_async_copy(
                source.at[half * VIRT + w, :, : OWNED * TILE], out_ref.at[half, :, tile_at(w * OWNED, OWNED)], sent
            ).start()

    for w in range(VIRT):
        pl.when(table_ref[HELD + w] == OWNED)(functools.partial(send, taken_ref, w))

    def mix(w):
        main = table_ref[MAIN + w]
        for half in range(2):
            mixed_ref[half * VIRT + w] = taken_ref[half * VIRT + w, :, : OWNED * TILE]

        @pl.loop(0, IRREPS)
        def _(irrep):
            first, count = table_ref[irrep], table_ref[IRREPS + irrep]
            size = clip_count(first, count, w)

            @pl.when((irrep != main) & (size > 0))
            def _():
                left_block, right_block = first // OWNED, (first + count - 1) // OWNED
                on_left = w == left_block
                low = jnp.where(on_left, left_block + 1, left_block)
                high = jnp.where(on_left, right_block + 1, right_block)
                start = OWNED + jnp.where(on_left, 0, table_ref[LEFT + irrep])
                slots = tile_at(jnp.minimum(start, OUT_SLOTS - SIDE), SIDE)
                offset = start - jnp.minimum(start, OUT_SLOTS - SIDE)

                def add(v, totals):
                    return tuple(
                        totals[half] + taken_ref[half * VIRT + v, :, slots].astype(jnp.float32) for half in range(2)
                    )

                zeros = jnp.zeros((ROWS, SIDE * TILE), jnp.float32)
                totals = lax.fori_loop(low, high, add, (zeros, zeros))
                for half in range(2):
                    total_ref[half] = totals[half]
                tile = jnp.maximum(first - w * OWNED, 0)

                @pl.loop(0, size)
                def _(at):
                    columns = tile_at(tile + at)
                    for half in range(2):
                        own = taken_ref[half * VIRT + w, :, columns].astype(jnp.float32)
                        total = own + total_ref[half, :, tile_at(offset + at)]
                        mixed_ref[half * VIRT + w, :, columns] = total.astype(jnp.bfloat16)

        send(mixed_ref, w)

    @pl.loop(0, VIRT)
    def _(w):
        pl.when(table_ref[HELD + w] < OWNED)(lambda: mix(w))

    pltpu.make_async_copy(out_ref, out_ref, sent).wait()


def collect(table, taken):
    out = pl.pallas_call(
        collect_kernel,
        out_shape=jax.ShapeDtypeStruct((2, ROWS, TILES * TILE), jnp.bfloat16),
        in_specs=[pl.BlockSpec(memory_space=pltpu.SMEM), pl.BlockSpec(memory_space=pltpu.VMEM)],
        out_specs=pl.BlockSpec(memory_space=pltpu.HBM),
        scratch_shapes=[
            pltpu.VMEM((2 * VIRT, ROWS, OWNED * TILE), jnp.bfloat16),
            pltpu.VMEM((2, ROWS, SIDE * TILE), jnp.float32),
            pltpu.SemaphoreType.DMA,
        ],
        compiler_params=pltpu.CompilerParams(vmem_limit_bytes=16 << 20),
        name="collect",
    )(table, taken)
    return out.reshape(2 * ROWS, TILES * TILE)


def on_device(amplitudes, tile_irreps, ladder_blocks):
    half = lax.axis_index("half")
    sent = lax.dynamic_slice_in_dim(amplitudes, (1 - half) * ROWS, ROWS, 0)
    own = lax.dynamic_slice_in_dim(amplitudes, half * ROWS, ROWS, 0)
    partner = lax.ppermute(sent, "half", [(0, 1), (1, 0)])
    place = jnp.stack([half, lax.axis_index("virt")]).astype(jnp.int32)
    table, near = plan(tile_irreps, ladder_blocks)
    table = jnp.concatenate([table, place])
    packed = pack(table, own, partner)
    taken = lax.all_to_all(packed, "virt", split_axis=0, concat_axis=0, tiled=True)
    sums = ladder(table, tile_irreps, taken, near)
    taken = lax.all_to_all(sums, ("half", "virt"), split_axis=0, concat_axis=0, tiled=True)
    return collect(table, taken)


def solution(mesh):
    pairs, virt = mesh.devices.shape
    split = Mesh(mesh.devices.reshape(2, pairs // 2, virt), ("half", "quarter", "virt"))
    rows = P(("half", "quarter", "virt"), None)
    return jax.shard_map(
        on_device, mesh=split, in_specs=(rows, P(), P("virt", None)), out_specs=rows, check_vma=False
    )
```

```python
import functools

import jax
import jax.numpy as jnp
from jax import lax
from jax.experimental import pallas as pl
from jax.experimental.pallas import tpu as pltpu
from jax.sharding import Mesh, PartitionSpec as P

TILE = 128
IRREPS = 4
TILES = 128
SECT = 48
OWNED = 8
VIRT = 16
ROWS = 8
EXTRA = 5
SLOTS = SECT + EXTRA
SIDE = 5
OUT_SLOTS = OWNED + SIDE
MAIN, HELD, LEFT, HALF, PLACE = 8, 24, 40, 44, 45


def clip_count(first, count, w):
    low, high = jnp.maximum(first, w * OWNED), jnp.minimum(first + count, w * OWNED + OWNED)
    return jnp.maximum(high - low, 0)


def plan_kernel(irreps_ref, blocks_ref, table_ref, near_ref, copied):
    copy = pltpu.make_async_copy(blocks_ref, near_ref, copied)
    copy.start()

    def count(at, counts):
        irrep = irreps_ref[at]
        return tuple(counts[g] + (irrep == g).astype(jnp.int32) for g in range(IRREPS))

    counts = lax.fori_loop(0, TILES, count, (jnp.int32(0),) * IRREPS)
    first = jnp.int32(0)
    firsts = []
    for g in range(IRREPS):
        firsts.append(first)
        table_ref[g] = first
        table_ref[IRREPS + g] = counts[g]
        first = first + counts[g]
    for w in range(VIRT):
        best, main = clip_count(firsts[0], counts[0], w), jnp.int32(0)
        for g in range(1, IRREPS):
            held = clip_count(firsts[g], counts[g], w)
            main = jnp.where(held >= best, g, main)
            best = jnp.maximum(held, best)
        table_ref[MAIN + w] = main
        table_ref[HELD + w] = best

    def ends(g):
        left_block = jnp.minimum(firsts[g] // OWNED, VIRT - 1)
        right_block = jnp.maximum(firsts[g] + counts[g] - 1, 0) // OWNED
        wide = (counts[g] > 0) & (left_block != right_block)
        left = jnp.where(wide & (table_ref[MAIN + left_block] != g), (left_block + 1) * OWNED - firsts[g], 0)
        right = jnp.where(
            wide & (table_ref[MAIN + right_block] != g), firsts[g] + counts[g] - right_block * OWNED, 0
        )
        return right_block, left, right

    for g in range(IRREPS):
        right_block, left, right = ends(g)

        @pl.when(left + right > SIDE)
        def _():
            table_ref[MAIN + right_block] = jnp.int32(g)
            table_ref[HELD + right_block] = clip_count(firsts[g], counts[g], right_block)

    for g in range(IRREPS):
        table_ref[LEFT + g] = ends(g)[1]
    copy.wait()


def plan(tile_irreps, blocks):
    return pl.pallas_call(
        plan_kernel,
        out_shape=(jax.ShapeDtypeStruct((HALF,), jnp.int32), jax.ShapeDtypeStruct(blocks.shape, blocks.dtype)),
        in_specs=[pl.BlockSpec(memory_space=pltpu.SMEM), pl.BlockSpec(memory_space=pltpu.HBM)],
        out_specs=(pl.BlockSpec(memory_space=pltpu.SMEM), pl.BlockSpec(memory_space=pltpu.VMEM)),
        scratch_shapes=[pltpu.SemaphoreType.DMA],
        compiler_params=pltpu.CompilerParams(vmem_limit_bytes=37 << 20),
        cost_estimate=pl.CostEstimate(flops=0, bytes_accessed=2 * blocks.size * 2, transcendentals=0),
        name="plan",
    )(tile_irreps, blocks)


def position(table_ref, w):
    main = table_ref[MAIN + w]
    first, count = table_ref[main], table_ref[IRREPS + main]
    return main, first, count, jnp.maximum(first - w * OWNED, 0), table_ref[HELD + w]


def pack_kernel(table_ref, own_ref, partner_ref, out_ref, tau_ref):
    for tile in range(TILES):
        columns = pl.ds(tile * TILE, TILE)
        mine = own_ref[:, columns].astype(jnp.float32)
        other = partner_ref[:, columns].astype(jnp.float32)
        tau_ref[tile] = (0.5 * (mine - other)).astype(jnp.bfloat16)
    tau_ref[TILES:] = jnp.zeros((SECT, ROWS, TILE), jnp.bfloat16)

    @pl.loop(0, VIRT)
    def _(w):
        _, first, _, before, held = position(table_ref, w)
        out_ref[w, :SECT] = tau_ref[pl.ds(first, SECT)]
        for extra in range(EXTRA):
            at = jnp.where(extra < before, extra, extra + held)
            at = jnp.where(at < OWNED, w * OWNED + at, TILES)
            out_ref[w, SECT + extra] = tau_ref[at]


def pack(table, own, partner):
    return pl.pallas_call(
        pack_kernel,
        out_shape=jax.ShapeDtypeStruct((VIRT, SLOTS, ROWS, TILE), jnp.bfloat16),
        in_specs=[pl.BlockSpec(memory_space=pltpu.SMEM)] + [pl.BlockSpec(memory_space=pltpu.VMEM)] * 2,
        out_specs=pl.BlockSpec(memory_space=pltpu.VMEM),
        scratch_shapes=[pltpu.VMEM((TILES + SECT, ROWS, TILE), jnp.bfloat16)],
        compiler_params=pltpu.CompilerParams(vmem_limit_bytes=16 << 20),
        name="pack",
    )(table, own, partner)


GROUP = 2
SHORT = 32
NT = (((1,), (1,)), ((), ()))
NN = (((1,), (0,)), ((), ()))


def tile_at(index, count=1):
    start = index * TILE if isinstance(index, int) else pl.multiple_of(index * TILE, TILE)
    return pl.ds(start, count * TILE)


def right_start(first, last_block):
    return jnp.minimum(last_block * OWNED - first, SECT - SIDE)


def ladder_kernel(table_ref, irreps_ref, tau_ref, block_ref, out_ref, held_ref, some_ref, part_ref):
    half, w = table_ref[HALF], table_ref[PLACE]
    main, main_first, main_count, before, held = position(table_ref, w)
    sign = jnp.where(half == 1, -1.0, 1.0)

    for slot in range(SLOTS):
        for src in range(0, VIRT, 2):
            rows = jnp.concatenate([tau_ref[src, slot], tau_ref[src + 1, slot]], axis=0)
            held_ref[pl.ds(src * ROWS, 2 * ROWS), pl.ds(slot * TILE, TILE)] = rows

    def tau_of(tile):
        inside = w * OWNED + tile - main_first
        outside = SECT + jnp.where(tile < before, tile, tile - held)
        return held_ref[:, tile_at(jnp.where(irreps_ref[w * OWNED + tile] == main, inside, outside))]

    def send(slot, values):
        upper = (values * sign).astype(jnp.bfloat16)
        for dest in range(VIRT):
            rows = upper[dest * ROWS : (dest + 1) * ROWS]
            out_ref[dest, :, tile_at(slot)] = rows
            out_ref[VIRT + dest, :, tile_at(slot)] = -rows

    def multiply(depth):
        @pl.loop(main_count, depth)
        def _(slot):
            held_ref[:, tile_at(slot)] = jnp.zeros((VIRT * ROWS, TILE), jnp.bfloat16)

        for start in range(0, OWNED, GROUP):
            sums = lax.dot_general(
                block_ref[start * TILE : (start + GROUP) * TILE, : depth * TILE],
                held_ref[:, : depth * TILE],
                NT,
                preferred_element_type=jnp.float32,
            )
            for tile in range(GROUP):
                send(start + tile, sums[tile * TILE : (tile + 1) * TILE].T)

    pl.when(main_count <= SHORT)(lambda: multiply(SHORT))
    pl.when(main_count > SHORT)(lambda: multiply(SECT))

    @pl.when(held < OWNED)
    def _():
        @pl.loop(0, IRREPS)
        def _(irrep):
            first, count = table_ref[irrep], table_ref[IRREPS + irrep]
            low = jnp.maximum(first - w * OWNED, 0)
            size = clip_count(first, count, w)

            @pl.when((irrep != main) & (size > 0))
            def _():
                column = w * OWNED + low - first
                start = jnp.minimum(column, SECT - SIDE)
                row = jnp.minimum(low, OWNED - SIDE)
                some_ref[...] = jnp.zeros_like(some_ref)

                @pl.loop(0, size)
                def _(at):
                    some_ref[:, tile_at(column - start + at)] = tau_of(low + at)

                part_ref[...] = lax.dot_general(
                    some_ref[:, : SIDE * TILE],
                    block_ref[tile_at(row, SIDE), tile_at(start, SIDE)],
                    NT,
                    preferred_element_type=jnp.float32,
                )

                @pl.loop(0, size)
                def _(at):
                    send(low + at, part_ref[:, tile_at(low - row + at)])

    def side(edge, is_left):
        irrep = irreps_ref[w * OWNED + edge]
        first, count = table_ref[irrep], table_ref[IRREPS + irrep]
        block = (first if is_left else first + count - 1) // OWNED

        @pl.when((block != w) & (table_ref[MAIN + block] != irrep))
        def _():
            for tile in range(OWNED):
                inside = irreps_ref[w * OWNED + tile] == irrep

                @pl.when(inside)
                def _():
                    some_ref[:, tile * TILE : (tile + 1) * TILE] = tau_of(tile)

                @pl.when(jnp.logical_not(inside))
                def _():
                    some_ref[:, tile * TILE : (tile + 1) * TILE] = jnp.zeros((VIRT * ROWS, TILE), jnp.bfloat16)

            at = 0 if is_left else right_start(first, block)
            part_ref[...] = lax.dot_general(
                some_ref[...], block_ref[:, tile_at(at, SIDE)], NN, preferred_element_type=jnp.float32
            )
            low = 0 if is_left else block * OWNED - first - at
            size = table_ref[LEFT + irrep] if is_left else first + count - block * OWNED
            slot = OWNED if is_left else OUT_SLOTS - size

            @pl.loop(0, size)
            def _(tile):
                send(slot + tile, part_ref[:, tile_at(low + tile)])

    side(0, True)
    side(OWNED - 1, False)


def ladder(table, tile_irreps, taken, blocks):
    rows = VIRT * ROWS
    return pl.pallas_call(
        ladder_kernel,
        out_shape=jax.ShapeDtypeStruct((2 * VIRT, ROWS, OUT_SLOTS * TILE), jnp.bfloat16),
        in_specs=[pl.BlockSpec(memory_space=pltpu.SMEM)] * 2 + [pl.BlockSpec(memory_space=pltpu.VMEM)] * 2,
        out_specs=pl.BlockSpec(memory_space=pltpu.VMEM),
        scratch_shapes=[
            pltpu.VMEM((rows, SLOTS * TILE), jnp.bfloat16),
            pltpu.VMEM((rows, OWNED * TILE), jnp.bfloat16),
            pltpu.VMEM((rows, SIDE * TILE), jnp.float32),
        ],
        compiler_params=pltpu.CompilerParams(vmem_limit_bytes=24 << 20),
        cost_estimate=pl.CostEstimate(
            flops=2 * rows * SECT * TILE * OWNED * TILE, bytes_accessed=16 << 20, transcendentals=0
        ),
        name="ladder",
    )(table, tile_irreps, taken, blocks)


def collect_kernel(table_ref, taken_ref, out_ref, mixed_ref, total_ref, sent):
    def send(source, w):
        for half in range(2):
            pltpu.make_async_copy(
                source.at[half * VIRT + w, :, : OWNED * TILE], out_ref.at[half, :, tile_at(w * OWNED, OWNED)], sent
            ).start()

    for w in range(VIRT):
        pl.when(table_ref[HELD + w] == OWNED)(functools.partial(send, taken_ref, w))

    def mix(w):
        main = table_ref[MAIN + w]
        for half in range(2):
            mixed_ref[half * VIRT + w] = taken_ref[half * VIRT + w, :, : OWNED * TILE]

        @pl.loop(0, IRREPS)
        def _(irrep):
            first, count = table_ref[irrep], table_ref[IRREPS + irrep]
            size = clip_count(first, count, w)

            @pl.when((irrep != main) & (size > 0))
            def _():
                left_block, right_block = first // OWNED, (first + count - 1) // OWNED
                on_left = w == left_block
                low = jnp.where(on_left, left_block + 1, left_block)
                high = jnp.where(on_left, right_block + 1, right_block)
                offset = jnp.where(on_left, 0, SIDE - size)

                def add(v, totals):
                    return tuple(
                        totals[half] + taken_ref[half * VIRT + v, :, OWNED * TILE :].astype(jnp.float32) for half in range(2)
                    )

                zeros = jnp.zeros((ROWS, SIDE * TILE), jnp.float32)
                totals = lax.fori_loop(low, high, add, (zeros, zeros))
                for half in range(2):
                    total_ref[half] = totals[half]
                tile = jnp.maximum(first - w * OWNED, 0)

                @pl.loop(0, size)
                def _(at):
                    columns = tile_at(tile + at)
                    for half in range(2):
                        own = taken_ref[half * VIRT + w, :, columns].astype(jnp.float32)
                        total = own + total_ref[half, :, tile_at(offset + at)]
                        mixed_ref[half * VIRT + w, :, columns] = total.astype(jnp.bfloat16)

        send(mixed_ref, w)

    @pl.loop(0, VIRT)
    def _(w):
        pl.when(table_ref[HELD + w] < OWNED)(lambda: mix(w))

    pltpu.make_async_copy(out_ref, out_ref, sent).wait()


def collect(table, taken):
    out = pl.pallas_call(
        collect_kernel,
        out_shape=jax.ShapeDtypeStruct((2, ROWS, TILES * TILE), jnp.bfloat16),
        in_specs=[pl.BlockSpec(memory_space=pltpu.SMEM), pl.BlockSpec(memory_space=pltpu.VMEM)],
        out_specs=pl.BlockSpec(memory_space=pltpu.HBM),
        scratch_shapes=[
            pltpu.VMEM((2 * VIRT, ROWS, OWNED * TILE), jnp.bfloat16),
            pltpu.VMEM((2, ROWS, SIDE * TILE), jnp.float32),
            pltpu.SemaphoreType.DMA,
        ],
        compiler_params=pltpu.CompilerParams(vmem_limit_bytes=16 << 20),
        name="collect",
    )(table, taken)
    return out.reshape(2 * ROWS, TILES * TILE)


def on_device(amplitudes, tile_irreps, ladder_blocks):
    half = lax.axis_index("half")
    sent = lax.dynamic_slice_in_dim(amplitudes, (1 - half) * ROWS, ROWS, 0)
    own = lax.dynamic_slice_in_dim(amplitudes, half * ROWS, ROWS, 0)
    partner = lax.ppermute(sent, "half", [(0, 1), (1, 0)])
    place = jnp.stack([half, lax.axis_index("virt")]).astype(jnp.int32)
    table, near = plan(tile_irreps, ladder_blocks)
    table = jnp.concatenate([table, place])
    packed = pack(table, own, partner)
    taken = lax.all_to_all(packed, "virt", split_axis=0, concat_axis=0, tiled=True)
    sums = ladder(table, tile_irreps, taken, near)
    taken = lax.all_to_all(sums, ("half", "virt"), split_axis=0, concat_axis=0, tiled=True)
    return collect(table, taken)


def solution(mesh):
    pairs, virt = mesh.devices.shape
    split = Mesh(mesh.devices.reshape(2, pairs // 2, virt), ("half", "quarter", "virt"))
    rows = P(("half", "quarter", "virt"), None)
    return jax.shard_map(
        on_device, mesh=split, in_specs=(rows, P(), P("virt", None)), out_specs=rows, check_vma=False
    )
```

```python
import functools

import jax
import jax.numpy as jnp
from jax import lax
from jax.experimental import pallas as pl
from jax.experimental.pallas import tpu as pltpu
from jax.sharding import Mesh, PartitionSpec as P

TILE = 128
IRREPS = 4
TILES = 128
SECT = 48
OWNED = 8
VIRT = 16
ROWS = 8
EXTRA = 5
SLOTS = SECT + EXTRA
SIDE = 5
OUT_SLOTS = OWNED + SIDE
MAIN, HELD, LEFT, HALF, PLACE = 8, 24, 40, 44, 45


def clip_count(first, count, w):
    low, high = jnp.maximum(first, w * OWNED), jnp.minimum(first + count, w * OWNED + OWNED)
    return jnp.maximum(high - low, 0)


def plan_kernel(irreps_ref, blocks_ref, table_ref, near_ref, copied):
    copy = pltpu.make_async_copy(blocks_ref, near_ref, copied)
    copy.start()

    def count(at, counts):
        irrep = irreps_ref[at]
        return tuple(counts[g] + (irrep == g).astype(jnp.int32) for g in range(IRREPS))

    counts = lax.fori_loop(0, TILES, count, (jnp.int32(0),) * IRREPS)
    first = jnp.int32(0)
    firsts = []
    for g in range(IRREPS):
        firsts.append(first)
        table_ref[g] = first
        table_ref[IRREPS + g] = counts[g]
        first = first + counts[g]
    for w in range(VIRT):
        best, main = clip_count(firsts[0], counts[0], w), jnp.int32(0)
        for g in range(1, IRREPS):
            held = clip_count(firsts[g], counts[g], w)
            main = jnp.where(held >= best, g, main)
            best = jnp.maximum(held, best)
        table_ref[MAIN + w] = main
        table_ref[HELD + w] = best

    def ends(g):
        left_block = jnp.minimum(firsts[g] // OWNED, VIRT - 1)
        right_block = jnp.maximum(firsts[g] + counts[g] - 1, 0) // OWNED
        wide = (counts[g] > 0) & (left_block != right_block)
        left = jnp.where(wide & (table_ref[MAIN + left_block] != g), (left_block + 1) * OWNED - firsts[g], 0)
        right = jnp.where(
            wide & (table_ref[MAIN + right_block] != g), firsts[g] + counts[g] - right_block * OWNED, 0
        )
        return right_block, left, right

    for g in range(IRREPS):
        right_block, left, right = ends(g)

        @pl.when(left + right > SIDE)
        def _():
            table_ref[MAIN + right_block] = jnp.int32(g)
            table_ref[HELD + right_block] = clip_count(firsts[g], counts[g], right_block)

    for g in range(IRREPS):
        table_ref[LEFT + g] = ends(g)[1]
    copy.wait()


def plan(tile_irreps, blocks):
    return pl.pallas_call(
        plan_kernel,
        out_shape=(jax.ShapeDtypeStruct((HALF,), jnp.int32), jax.ShapeDtypeStruct(blocks.shape, blocks.dtype)),
        in_specs=[pl.BlockSpec(memory_space=pltpu.SMEM), pl.BlockSpec(memory_space=pltpu.HBM)],
        out_specs=(pl.BlockSpec(memory_space=pltpu.SMEM), pl.BlockSpec(memory_space=pltpu.VMEM)),
        scratch_shapes=[pltpu.SemaphoreType.DMA],
        compiler_params=pltpu.CompilerParams(vmem_limit_bytes=37 << 20),
        cost_estimate=pl.CostEstimate(flops=0, bytes_accessed=2 * blocks.size * 2, transcendentals=0),
        name="plan",
    )(tile_irreps, blocks)


def position(table_ref, w):
    main = table_ref[MAIN + w]
    first, count = table_ref[main], table_ref[IRREPS + main]
    return main, first, count, jnp.maximum(first - w * OWNED, 0), table_ref[HELD + w]


def pack_kernel(table_ref, own_ref, partner_ref, out_ref, tau_ref):
    for tile in range(TILES):
        columns = pl.ds(tile * TILE, TILE)
        mine = own_ref[:, columns].astype(jnp.float32)
        other = partner_ref[:, columns].astype(jnp.float32)
        tau_ref[tile] = (0.5 * (mine - other)).astype(jnp.bfloat16)
    tau_ref[TILES:] = jnp.zeros((SECT, ROWS, TILE), jnp.bfloat16)

    @pl.loop(0, VIRT)
    def _(w):
        _, first, _, before, held = position(table_ref, w)
        out_ref[w, :SECT] = tau_ref[pl.ds(first, SECT)]
        for extra in range(EXTRA):
            at = jnp.where(extra < before, extra, extra + held)
            at = jnp.where(at < OWNED, w * OWNED + at, TILES)
            out_ref[w, SECT + extra] = tau_ref[at]


def pack(table, own, partner):
    return pl.pallas_call(
        pack_kernel,
        out_shape=jax.ShapeDtypeStruct((VIRT, SLOTS, ROWS, TILE), jnp.bfloat16),
        in_specs=[pl.BlockSpec(memory_space=pltpu.SMEM)] + [pl.BlockSpec(memory_space=pltpu.VMEM)] * 2,
        out_specs=pl.BlockSpec(memory_space=pltpu.VMEM),
        scratch_shapes=[pltpu.VMEM((TILES + SECT, ROWS, TILE), jnp.bfloat16)],
        compiler_params=pltpu.CompilerParams(vmem_limit_bytes=16 << 20),
        name="pack",
    )(table, own, partner)


GROUP = 2
NARROW = 3
SHORT = 32
NT = (((1,), (1,)), ((), ()))
NN = (((1,), (0,)), ((), ()))


def tile_at(index, count=1):
    start = index * TILE if isinstance(index, int) else pl.multiple_of(index * TILE, TILE)
    return pl.ds(start, count * TILE)


def ladder_kernel(table_ref, irreps_ref, tau_ref, block_ref, out_ref, held_ref, some_ref, part_ref):
    half, w = table_ref[HALF], table_ref[PLACE]
    main, main_first, main_count, before, held = position(table_ref, w)
    sign = jnp.where(half == 1, -1.0, 1.0)

    for slot in range(SLOTS):
        for src in range(0, VIRT, 2):
            rows = jnp.concatenate([tau_ref[src, slot], tau_ref[src + 1, slot]], axis=0)
            held_ref[pl.ds(src * ROWS, 2 * ROWS), pl.ds(slot * TILE, TILE)] = rows

    def tau_of(tile):
        inside = w * OWNED + tile - main_first
        outside = SECT + jnp.where(tile < before, tile, tile - held)
        return held_ref[:, tile_at(jnp.where(irreps_ref[w * OWNED + tile] == main, inside, outside))]

    def send(slot, values):
        upper = (values * sign).astype(jnp.bfloat16)
        for dest in range(VIRT):
            rows = upper[dest * ROWS : (dest + 1) * ROWS]
            out_ref[dest, :, tile_at(slot)] = rows
            out_ref[VIRT + dest, :, tile_at(slot)] = -rows

    def multiply(depth):
        @pl.loop(main_count, depth)
        def _(slot):
            held_ref[:, tile_at(slot)] = jnp.zeros((VIRT * ROWS, TILE), jnp.bfloat16)

        for start in range(0, OWNED, GROUP):
            sums = lax.dot_general(
                block_ref[start * TILE : (start + GROUP) * TILE, : depth * TILE],
                held_ref[:, : depth * TILE],
                NT,
                preferred_element_type=jnp.float32,
            )
            for tile in range(GROUP):
                send(start + tile, sums[tile * TILE : (tile + 1) * TILE].T)

    pl.when(main_count <= SHORT)(lambda: multiply(SHORT))
    pl.when(main_count > SHORT)(lambda: multiply(SECT))

    @pl.when(held < OWNED)
    def _():
        @pl.loop(0, IRREPS)
        def _(irrep):
            first, count = table_ref[irrep], table_ref[IRREPS + irrep]
            low = jnp.maximum(first - w * OWNED, 0)
            size = clip_count(first, count, w)

            def piece(width):
                column = w * OWNED + low - first
                start = jnp.minimum(column, SECT - width)
                row = jnp.minimum(low, OWNED - width)
                some_ref[:, : width * TILE] = jnp.zeros((VIRT * ROWS, width * TILE), jnp.bfloat16)

                @pl.loop(0, size)
                def _(at):
                    some_ref[:, tile_at(column - start + at)] = tau_of(low + at)

                part_ref[:, : width * TILE] = lax.dot_general(
                    some_ref[:, : width * TILE],
                    block_ref[tile_at(row, width), tile_at(start, width)],
                    NT,
                    preferred_element_type=jnp.float32,
                )

                @pl.loop(0, size)
                def _(at):
                    send(low + at, part_ref[:, tile_at(low - row + at)])

            pl.when((irrep != main) & (size > 0) & (size <= NARROW))(lambda: piece(NARROW))
            pl.when((irrep != main) & (size > NARROW))(lambda: piece(SIDE))

    def side(edge, is_left):
        irrep = irreps_ref[w * OWNED + edge]
        first, count = table_ref[irrep], table_ref[IRREPS + irrep]
        block = (first if is_left else first + count - 1) // OWNED
        size = table_ref[LEFT + irrep] if is_left else first + count - block * OWNED
        slot = OWNED if is_left else OUT_SLOTS - size
        on = (block != w) & (table_ref[MAIN + block] != irrep)

        def partial(width):
            for tile in range(OWNED):
                inside = irreps_ref[w * OWNED + tile] == irrep
                values = tau_of(tile)
                some_ref[:, tile * TILE : (tile + 1) * TILE] = jnp.where(inside, values, jnp.zeros_like(values))
            column = 0 if is_left else block * OWNED - first
            start = 0 if is_left else jnp.minimum(column, SECT - width)
            part_ref[:, : width * TILE] = lax.dot_general(
                some_ref[...], block_ref[:, tile_at(start, width)], NN, preferred_element_type=jnp.float32
            )

            @pl.loop(0, size)
            def _(tile):
                send(slot + tile, part_ref[:, tile_at(column - start + tile)])

        pl.when(on & (size <= NARROW))(lambda: partial(NARROW))
        pl.when(on & (size > NARROW))(lambda: partial(SIDE))

    side(0, True)
    side(OWNED - 1, False)


def ladder(table, tile_irreps, taken, blocks):
    rows = VIRT * ROWS
    return pl.pallas_call(
        ladder_kernel,
        out_shape=jax.ShapeDtypeStruct((2 * VIRT, ROWS, OUT_SLOTS * TILE), jnp.bfloat16),
        in_specs=[pl.BlockSpec(memory_space=pltpu.SMEM)] * 2 + [pl.BlockSpec(memory_space=pltpu.VMEM)] * 2,
        out_specs=pl.BlockSpec(memory_space=pltpu.VMEM),
        scratch_shapes=[
            pltpu.VMEM((rows, SLOTS * TILE), jnp.bfloat16),
            pltpu.VMEM((rows, OWNED * TILE), jnp.bfloat16),
            pltpu.VMEM((rows, SIDE * TILE), jnp.float32),
        ],
        compiler_params=pltpu.CompilerParams(vmem_limit_bytes=24 << 20),
        cost_estimate=pl.CostEstimate(
            flops=2 * rows * SECT * TILE * OWNED * TILE, bytes_accessed=16 << 20, transcendentals=0
        ),
        name="ladder",
    )(table, tile_irreps, taken, blocks)


def collect_kernel(table_ref, taken_ref, out_ref, mixed_ref, total_ref, sent):
    def send(source, w):
        for half in range(2):
            pltpu.make_async_copy(
                source.at[half * VIRT + w, :, : OWNED * TILE], out_ref.at[half, :, tile_at(w * OWNED, OWNED)], sent
            ).start()

    for w in range(VIRT):
        pl.when(table_ref[HELD + w] == OWNED)(functools.partial(send, taken_ref, w))

    def mix(w):
        main = table_ref[MAIN + w]
        for half in range(2):
            mixed_ref[half * VIRT + w] = taken_ref[half * VIRT + w, :, : OWNED * TILE]

        @pl.loop(0, IRREPS)
        def _(irrep):
            first, count = table_ref[irrep], table_ref[IRREPS + irrep]
            size = clip_count(first, count, w)

            @pl.when((irrep != main) & (size > 0))
            def _():
                left_block, right_block = first // OWNED, (first + count - 1) // OWNED
                on_left = w == left_block
                low = jnp.where(on_left, left_block + 1, left_block)
                high = jnp.where(on_left, right_block + 1, right_block)
                offset = jnp.where(on_left, 0, SIDE - size)

                def add(v, totals):
                    return tuple(
                        totals[half] + taken_ref[half * VIRT + v, :, OWNED * TILE :].astype(jnp.float32) for half in range(2)
                    )

                zeros = jnp.zeros((ROWS, SIDE * TILE), jnp.float32)
                totals = lax.fori_loop(low, high, add, (zeros, zeros))
                for half in range(2):
                    total_ref[half] = totals[half]
                tile = jnp.maximum(first - w * OWNED, 0)

                @pl.loop(0, size)
                def _(at):
                    columns = tile_at(tile + at)
                    for half in range(2):
                        own = taken_ref[half * VIRT + w, :, columns].astype(jnp.float32)
                        total = own + total_ref[half, :, tile_at(offset + at)]
                        mixed_ref[half * VIRT + w, :, columns] = total.astype(jnp.bfloat16)

        send(mixed_ref, w)

    @pl.loop(0, VIRT)
    def _(w):
        pl.when(table_ref[HELD + w] < OWNED)(lambda: mix(w))

    pltpu.make_async_copy(out_ref, out_ref, sent).wait()


def collect(table, taken):
    out = pl.pallas_call(
        collect_kernel,
        out_shape=jax.ShapeDtypeStruct((2, ROWS, TILES * TILE), jnp.bfloat16),
        in_specs=[pl.BlockSpec(memory_space=pltpu.SMEM), pl.BlockSpec(memory_space=pltpu.VMEM)],
        out_specs=pl.BlockSpec(memory_space=pltpu.HBM),
        scratch_shapes=[
            pltpu.VMEM((2 * VIRT, ROWS, OWNED * TILE), jnp.bfloat16),
            pltpu.VMEM((2, ROWS, SIDE * TILE), jnp.float32),
            pltpu.SemaphoreType.DMA,
        ],
        compiler_params=pltpu.CompilerParams(vmem_limit_bytes=16 << 20),
        name="collect",
    )(table, taken)
    return out.reshape(2 * ROWS, TILES * TILE)


def on_device(amplitudes, tile_irreps, ladder_blocks):
    half = lax.axis_index("half")
    sent = lax.dynamic_slice_in_dim(amplitudes, (1 - half) * ROWS, ROWS, 0)
    own = lax.dynamic_slice_in_dim(amplitudes, half * ROWS, ROWS, 0)
    partner = lax.ppermute(sent, "half", [(0, 1), (1, 0)])
    place = jnp.stack([half, lax.axis_index("virt")]).astype(jnp.int32)
    table, near = plan(tile_irreps, ladder_blocks)
    table = jnp.concatenate([table, place])
    packed = pack(table, own, partner)
    taken = lax.all_to_all(packed, "virt", split_axis=0, concat_axis=0, tiled=True)
    sums = ladder(table, tile_irreps, taken, near)
    taken = lax.all_to_all(sums, ("half", "virt"), split_axis=0, concat_axis=0, tiled=True)
    return collect(table, taken)


def solution(mesh):
    pairs, virt = mesh.devices.shape
    split = Mesh(mesh.devices.reshape(2, pairs // 2, virt), ("half", "quarter", "virt"))
    rows = P(("half", "quarter", "virt"), None)
    return jax.shard_map(
        on_device, mesh=split, in_specs=(rows, P(), P("virt", None)), out_specs=rows, check_vma=False
    )
```

```python
import functools

import jax
import jax.numpy as jnp
from jax import lax
from jax.experimental import pallas as pl
from jax.experimental.pallas import tpu as pltpu
from jax.sharding import Mesh, PartitionSpec as P

TILE = 128
IRREPS = 4
TILES = 128
SECT = 48
OWNED = 8
VIRT = 16
ROWS = 8
EXTRA = 5
SLOTS = SECT + EXTRA
SIDE = 5
OUT_SLOTS = OWNED + SIDE
MAIN, HELD, LEFT, HALF, PLACE = 8, 24, 40, 44, 45


def clip_count(first, count, w):
    low, high = jnp.maximum(first, w * OWNED), jnp.minimum(first + count, w * OWNED + OWNED)
    return jnp.maximum(high - low, 0)


def plan_kernel(irreps_ref, blocks_ref, table_ref, near_ref, copied):
    copy = pltpu.make_async_copy(blocks_ref, near_ref, copied)
    copy.start()

    def count(at, counts):
        irrep = irreps_ref[at]
        return tuple(counts[g] + (irrep == g).astype(jnp.int32) for g in range(IRREPS))

    counts = lax.fori_loop(0, TILES, count, (jnp.int32(0),) * IRREPS)
    first = jnp.int32(0)
    firsts = []
    for g in range(IRREPS):
        firsts.append(first)
        table_ref[g] = first
        table_ref[IRREPS + g] = counts[g]
        first = first + counts[g]
    for w in range(VIRT):
        best, main = clip_count(firsts[0], counts[0], w), jnp.int32(0)
        for g in range(1, IRREPS):
            held = clip_count(firsts[g], counts[g], w)
            main = jnp.where(held >= best, g, main)
            best = jnp.maximum(held, best)
        table_ref[MAIN + w] = main
        table_ref[HELD + w] = best

    def ends(g):
        left_block = jnp.minimum(firsts[g] // OWNED, VIRT - 1)
        right_block = jnp.maximum(firsts[g] + counts[g] - 1, 0) // OWNED
        wide = (counts[g] > 0) & (left_block != right_block)
        left = jnp.where(wide & (table_ref[MAIN + left_block] != g), (left_block + 1) * OWNED - firsts[g], 0)
        right = jnp.where(
            wide & (table_ref[MAIN + right_block] != g), firsts[g] + counts[g] - right_block * OWNED, 0
        )
        return right_block, left, right

    for g in range(IRREPS):
        right_block, left, right = ends(g)

        @pl.when(left + right > SIDE)
        def _():
            table_ref[MAIN + right_block] = jnp.int32(g)
            table_ref[HELD + right_block] = clip_count(firsts[g], counts[g], right_block)

    for g in range(IRREPS):
        table_ref[LEFT + g] = ends(g)[1]
    copy.wait()


def plan(tile_irreps, blocks):
    return pl.pallas_call(
        plan_kernel,
        out_shape=(jax.ShapeDtypeStruct((HALF,), jnp.int32), jax.ShapeDtypeStruct(blocks.shape, blocks.dtype)),
        in_specs=[pl.BlockSpec(memory_space=pltpu.SMEM), pl.BlockSpec(memory_space=pltpu.HBM)],
        out_specs=(pl.BlockSpec(memory_space=pltpu.SMEM), pl.BlockSpec(memory_space=pltpu.VMEM)),
        scratch_shapes=[pltpu.SemaphoreType.DMA],
        compiler_params=pltpu.CompilerParams(vmem_limit_bytes=37 << 20),
        cost_estimate=pl.CostEstimate(flops=0, bytes_accessed=2 * blocks.size * 2, transcendentals=0),
        name="plan",
    )(tile_irreps, blocks)


def position(table_ref, w):
    main = table_ref[MAIN + w]
    first, count = table_ref[main], table_ref[IRREPS + main]
    return main, first, count, jnp.maximum(first - w * OWNED, 0), table_ref[HELD + w]


def pack_kernel(table_ref, own_ref, partner_ref, out_ref, tau_ref):
    for tile in range(TILES):
        columns = pl.ds(tile * TILE, TILE)
        mine = own_ref[:, columns].astype(jnp.float32)
        other = partner_ref[:, columns].astype(jnp.float32)
        tau_ref[tile] = (0.5 * (mine - other)).astype(jnp.bfloat16)
    tau_ref[TILES:] = jnp.zeros((SECT, ROWS, TILE), jnp.bfloat16)

    @pl.loop(0, VIRT)
    def _(w):
        _, first, _, before, held = position(table_ref, w)
        out_ref[w, :SECT] = tau_ref[pl.ds(first, SECT)]
        for extra in range(EXTRA):
            at = jnp.where(extra < before, extra, extra + held)
            at = jnp.where(at < OWNED, w * OWNED + at, TILES)
            out_ref[w, SECT + extra] = tau_ref[at]


def pack(table, own, partner):
    return pl.pallas_call(
        pack_kernel,
        out_shape=jax.ShapeDtypeStruct((VIRT, SLOTS, ROWS, TILE), jnp.bfloat16),
        in_specs=[pl.BlockSpec(memory_space=pltpu.SMEM)] + [pl.BlockSpec(memory_space=pltpu.VMEM)] * 2,
        out_specs=pl.BlockSpec(memory_space=pltpu.VMEM),
        scratch_shapes=[pltpu.VMEM((TILES + SECT, ROWS, TILE), jnp.bfloat16)],
        compiler_params=pltpu.CompilerParams(vmem_limit_bytes=16 << 20),
        name="pack",
    )(table, own, partner)


GROUP = 2
NARROW = 3
SHORT = 32
NT = (((1,), (1,)), ((), ()))
NN = (((1,), (0,)), ((), ()))


def tile_at(index, count=1):
    start = index * TILE if isinstance(index, int) else pl.multiple_of(index * TILE, TILE)
    return pl.ds(start, count * TILE)


def ladder_kernel(table_ref, irreps_ref, tau_ref, block_ref, out_ref, held_ref, some_ref, part_ref):
    half, w = table_ref[HALF], table_ref[PLACE]
    main, main_first, main_count, before, held = position(table_ref, w)
    sign = jnp.where(half == 1, -1.0, 1.0)

    for slot in range(SLOTS):
        for src in range(0, VIRT, 2):
            rows = jnp.concatenate([tau_ref[src, slot], tau_ref[src + 1, slot]], axis=0)
            held_ref[pl.ds(src * ROWS, 2 * ROWS), pl.ds(slot * TILE, TILE)] = rows

    def tau_of(tile):
        inside = w * OWNED + tile - main_first
        outside = SECT + jnp.where(tile < before, tile, tile - held)
        return held_ref[:, tile_at(jnp.where(irreps_ref[w * OWNED + tile] == main, inside, outside))]

    def send(slot, values):
        upper = (values * sign).astype(jnp.bfloat16)
        for dest in range(VIRT):
            rows = upper[dest * ROWS : (dest + 1) * ROWS]
            out_ref[dest, :, tile_at(slot)] = rows
            out_ref[VIRT + dest, :, tile_at(slot)] = -rows

    def multiply(depth):
        @pl.loop(main_count, depth)
        def _(slot):
            held_ref[:, tile_at(slot)] = jnp.zeros((VIRT * ROWS, TILE), jnp.bfloat16)

        def group(start):
            sums = lax.dot_general(
                block_ref[tile_at(start, GROUP), : depth * TILE],
                held_ref[:, : depth * TILE],
                NT,
                preferred_element_type=jnp.float32,
            )
            for tile in range(GROUP):
                send(start + tile, sums[tile * TILE : (tile + 1) * TILE].T)

        @pl.when(held == OWNED)
        def _():
            for start in range(0, OWNED, GROUP):
                group(start)

        @pl.when(held < OWNED)
        def _():
            pl.loop(before // GROUP, (before + held + GROUP - 1) // GROUP)(lambda at: group(at * GROUP))

    pl.when(main_count <= SHORT)(lambda: multiply(SHORT))
    pl.when(main_count > SHORT)(lambda: multiply(SECT))

    @pl.when(held < OWNED)
    def _():
        @pl.loop(0, IRREPS)
        def _(irrep):
            first, count = table_ref[irrep], table_ref[IRREPS + irrep]
            low = jnp.maximum(first - w * OWNED, 0)
            size = clip_count(first, count, w)

            def piece(width):
                column = w * OWNED + low - first
                start = jnp.minimum(column, SECT - width)
                row = jnp.minimum(low, OWNED - width)
                some_ref[:, : width * TILE] = jnp.zeros((VIRT * ROWS, width * TILE), jnp.bfloat16)

                @pl.loop(0, size)
                def _(at):
                    some_ref[:, tile_at(column - start + at)] = tau_of(low + at)

                part_ref[:, : width * TILE] = lax.dot_general(
                    some_ref[:, : width * TILE],
                    block_ref[tile_at(row, width), tile_at(start, width)],
                    NT,
                    preferred_element_type=jnp.float32,
                )

                @pl.loop(0, size)
                def _(at):
                    send(low + at, part_ref[:, tile_at(low - row + at)])

            pl.when((irrep != main) & (size > 0) & (size <= NARROW))(lambda: piece(NARROW))
            pl.when((irrep != main) & (size > NARROW))(lambda: piece(SIDE))

    def side(edge, is_left):
        irrep = irreps_ref[w * OWNED + edge]
        first, count = table_ref[irrep], table_ref[IRREPS + irrep]
        block = (first if is_left else first + count - 1) // OWNED
        size = table_ref[LEFT + irrep] if is_left else first + count - block * OWNED
        slot = OWNED if is_left else OUT_SLOTS - size
        on = (block != w) & (table_ref[MAIN + block] != irrep)

        def partial(width):
            for tile in range(OWNED):
                inside = irreps_ref[w * OWNED + tile] == irrep
                values = tau_of(tile)
                some_ref[:, tile * TILE : (tile + 1) * TILE] = jnp.where(inside, values, jnp.zeros_like(values))
            column = 0 if is_left else block * OWNED - first
            start = 0 if is_left else jnp.minimum(column, SECT - width)
            part_ref[:, : width * TILE] = lax.dot_general(
                some_ref[...], block_ref[:, tile_at(start, width)], NN, preferred_element_type=jnp.float32
            )

            @pl.loop(0, size)
            def _(tile):
                send(slot + tile, part_ref[:, tile_at(column - start + tile)])

        pl.when(on & (size <= NARROW))(lambda: partial(NARROW))
        pl.when(on & (size > NARROW))(lambda: partial(SIDE))

    side(0, True)
    side(OWNED - 1, False)


def ladder(table, tile_irreps, taken, blocks):
    rows = VIRT * ROWS
    return pl.pallas_call(
        ladder_kernel,
        out_shape=jax.ShapeDtypeStruct((2 * VIRT, ROWS, OUT_SLOTS * TILE), jnp.bfloat16),
        in_specs=[pl.BlockSpec(memory_space=pltpu.SMEM)] * 2 + [pl.BlockSpec(memory_space=pltpu.VMEM)] * 2,
        out_specs=pl.BlockSpec(memory_space=pltpu.VMEM),
        scratch_shapes=[
            pltpu.VMEM((rows, SLOTS * TILE), jnp.bfloat16),
            pltpu.VMEM((rows, OWNED * TILE), jnp.bfloat16),
            pltpu.VMEM((rows, SIDE * TILE), jnp.float32),
        ],
        compiler_params=pltpu.CompilerParams(vmem_limit_bytes=24 << 20),
        cost_estimate=pl.CostEstimate(
            flops=2 * rows * SECT * TILE * OWNED * TILE, bytes_accessed=16 << 20, transcendentals=0
        ),
        name="ladder",
    )(table, tile_irreps, taken, blocks)


def collect_kernel(table_ref, taken_ref, out_ref, mixed_ref, total_ref, sent):
    def send(source, w):
        for half in range(2):
            pltpu.make_async_copy(
                source.at[half * VIRT + w, :, : OWNED * TILE], out_ref.at[half, :, tile_at(w * OWNED, OWNED)], sent
            ).start()

    for w in range(VIRT):
        pl.when(table_ref[HELD + w] == OWNED)(functools.partial(send, taken_ref, w))

    def mix(w):
        main = table_ref[MAIN + w]
        for half in range(2):
            mixed_ref[half * VIRT + w] = taken_ref[half * VIRT + w, :, : OWNED * TILE]

        @pl.loop(0, IRREPS)
        def _(irrep):
            first, count = table_ref[irrep], table_ref[IRREPS + irrep]
            size = clip_count(first, count, w)

            @pl.when((irrep != main) & (size > 0))
            def _():
                left_block, right_block = first // OWNED, (first + count - 1) // OWNED
                on_left = w == left_block
                low = jnp.where(on_left, left_block + 1, left_block)
                high = jnp.where(on_left, right_block + 1, right_block)
                offset = jnp.where(on_left, 0, SIDE - size)

                def add(v, totals):
                    return tuple(
                        totals[half] + taken_ref[half * VIRT + v, :, OWNED * TILE :].astype(jnp.float32) for half in range(2)
                    )

                zeros = jnp.zeros((ROWS, SIDE * TILE), jnp.float32)
                totals = lax.fori_loop(low, high, add, (zeros, zeros))
                for half in range(2):
                    total_ref[half] = totals[half]
                tile = jnp.maximum(first - w * OWNED, 0)

                @pl.loop(0, size)
                def _(at):
                    columns = tile_at(tile + at)
                    for half in range(2):
                        own = taken_ref[half * VIRT + w, :, columns].astype(jnp.float32)
                        total = own + total_ref[half, :, tile_at(offset + at)]
                        mixed_ref[half * VIRT + w, :, columns] = total.astype(jnp.bfloat16)

        send(mixed_ref, w)

    @pl.loop(0, VIRT)
    def _(w):
        pl.when(table_ref[HELD + w] < OWNED)(lambda: mix(w))

    pltpu.make_async_copy(out_ref, out_ref, sent).wait()


def collect(table, taken):
    out = pl.pallas_call(
        collect_kernel,
        out_shape=jax.ShapeDtypeStruct((2, ROWS, TILES * TILE), jnp.bfloat16),
        in_specs=[pl.BlockSpec(memory_space=pltpu.SMEM), pl.BlockSpec(memory_space=pltpu.VMEM)],
        out_specs=pl.BlockSpec(memory_space=pltpu.HBM),
        scratch_shapes=[
            pltpu.VMEM((2 * VIRT, ROWS, OWNED * TILE), jnp.bfloat16),
            pltpu.VMEM((2, ROWS, SIDE * TILE), jnp.float32),
            pltpu.SemaphoreType.DMA,
        ],
        compiler_params=pltpu.CompilerParams(vmem_limit_bytes=16 << 20),
        name="collect",
    )(table, taken)
    return out.reshape(2 * ROWS, TILES * TILE)


def on_device(amplitudes, tile_irreps, ladder_blocks):
    half = lax.axis_index("half")
    sent = lax.dynamic_slice_in_dim(amplitudes, (1 - half) * ROWS, ROWS, 0)
    own = lax.dynamic_slice_in_dim(amplitudes, half * ROWS, ROWS, 0)
    partner = lax.ppermute(sent, "half", [(0, 1), (1, 0)])
    place = jnp.stack([half, lax.axis_index("virt")]).astype(jnp.int32)
    table, near = plan(tile_irreps, ladder_blocks)
    table = jnp.concatenate([table, place])
    packed = pack(table, own, partner)
    taken = lax.all_to_all(packed, "virt", split_axis=0, concat_axis=0, tiled=True)
    sums = ladder(table, tile_irreps, taken, near)
    taken = lax.all_to_all(sums, ("half", "virt"), split_axis=0, concat_axis=0, tiled=True)
    return collect(table, taken)


def solution(mesh):
    pairs, virt = mesh.devices.shape
    split = Mesh(mesh.devices.reshape(2, pairs // 2, virt), ("half", "quarter", "virt"))
    rows = P(("half", "quarter", "virt"), None)
    return jax.shard_map(
        on_device, mesh=split, in_specs=(rows, P(), P("virt", None)), out_specs=rows, check_vma=False
    )
```
